32 devices in a mesh: gx: 8 (over z, x), gy: 4 (over y, core).
Axes of the slice: x: 2, y: 2, z: 4, core: 2. Of those that a mesh axis runs over, the one named last changes fastest.
Arguments:
- probes: bfloat16 [64, 64, 64, 128], P(None, 'gx', 'gy'), may hold values from -6 to 6
- permeability: float32 [64, 64, 128], P('gx', 'gy'), may hold values from 0.2 to 5
- absorption: float32 [64, 64, 128], P('gx', 'gy'), may hold values from 0.3 to 3
- sensitivity: float32 [64, 64, 128], P('gx', 'gy'), may hold values from -6 to 6
- observe_weight: float32 [64, 64, 128], P('gx', 'gy'), may hold values from 1 to 10
Outputs:
- q_basis: float32 [64, 64, 64, 128], P(None, 'gx', 'gy')
- r_factor: float32 [64, 64], replicated
The draws below stay inside these ranges and needn't reach their ends.
All inputs are finite; a program needn't handle non-finite values.
Results may differ from the reference program's by a relative error of at most 0.0003.
Values sent between devices are 32-bit elements; how exact they have to be, the bound alone decides.
No kernel may reach another device: no remote copies, remote signals or barrier semaphores. Data moves between devices by JAX's collectives and lax.ppermute only.
A program may use at most 128 MiB of HBM per device.

```python
import math
import jax
import jax.numpy as jnp
from jax import lax

PROBES = 64
SWEEPS = 4
NX = 64
NY = 64
NZ = 128


def shard_levels(rng, dims, cuts, low, top_value):
    def one(position, blocks):
        steps = jax.random.uniform(jax.random.fold_in(jax.random.fold_in(rng, 6), position), (blocks,), jnp.float32, low / len(cuts), top_value / len(cuts))
        return jnp.repeat(jnp.exp(steps), dims[position] // blocks).reshape((-1,) + (1,) * (len(dims) - position - 1))

    level = one(*cuts[0])
    for cut in cuts[1:]:
        level = level * one(*cut)
    return level


def bell_draw(key, dims, spread, reach, pieces=(), held_as=jnp.bfloat16):
    drawn = spread * jax.random.normal(key, dims, jnp.float32)
    if pieces:
        drawn = drawn * shard_levels(key, dims, pieces, -0.22, 0.18)
    return jnp.clip(drawn, -reach, reach).astype(held_as)


def setup_inputs(seed: int = 0) -> dict:
    splits = jax.random.split(jax.random.key(seed), 6)
    probes = bell_draw(splits[0], (PROBES, NX, NY, NZ), 1.0, 6.0, ((1, 8), (2, 4)))
    permeability = jnp.clip(jnp.exp(math.log(5.0) - 3.218876 * jax.random.uniform(splits[1], (NX, NY, NZ), jnp.float32) ** shard_levels(splits[1], (NX, NY, NZ), ((0, 8), (1, 4)), -0.2, 0.2)), 0.2, 5.0)
    absorption = jnp.clip(jnp.exp(math.log(3.0) - 2.3025851 * jax.random.uniform(splits[2], (NX, NY, NZ), jnp.float32) ** shard_levels(splits[2], (NX, NY, NZ), ((0, 8), (1, 4)), -0.2, 0.2)), 0.3, 3.0)
    sensitivity = bell_draw(splits[3], (NX, NY, NZ), 1.0, 6.0, ((0, 8), (1, 4)), jnp.float32)
    observe_weight = jnp.clip(jnp.exp(math.log(10.0) - 2.3025851 * jax.random.uniform(splits[4], (NX, NY, NZ), jnp.float32) ** shard_levels(splits[4], (NX, NY, NZ), ((0, 8), (1, 4)), -0.2, 0.2)), 1.0, 10.0)
    return {"probes": probes, "permeability": permeability, "absorption": absorption, "sensitivity": sensitivity, "observe_weight": observe_weight}


def face_terms(kpad, absorption):
    center = kpad[1:-1, 1:-1]
    x_low = 0.5 * (center + kpad[:-2, 1:-1])
    x_high = 0.5 * (center + kpad[2:, 1:-1])
    y_low = 0.5 * (center + kpad[1:-1, :-2])
    y_high = 0.5 * (center + kpad[1:-1, 2:])
    zpad = jnp.pad(center, ((0, 0), (0, 0), (1, 1)))
    z_low = 0.5 * (center + zpad[:, :, :-2])
    z_high = 0.5 * (center + zpad[:, :, 2:])
    diag = absorption + x_low + x_high + y_low + y_high + z_low + z_high
    return ((x_low, x_high, y_low, y_high, z_low, z_high), diag)

def sweep(field, padded, rhs, coefs, diag):
    x_low, x_high, y_low, y_high, z_low, z_high = coefs
    zpad = jnp.pad(field, ((0, 0), (0, 0), (0, 0), (1, 1)))
    total = x_low * padded[:, :-2, 1:-1] + x_high * padded[:, 2:, 1:-1]
    total = total + y_low * padded[:, 1:-1, :-2] + y_high * padded[:, 1:-1, 2:]
    total = total + z_low * zpad[..., :-2] + z_high * zpad[..., 2:]
    return 0.2 * field + 0.8 * (rhs + total) / diag

def jacobi(rhs, coefs, diag):
    field = jnp.zeros_like(rhs)
    for step in range(SWEEPS):
        padded = jnp.pad(field, ((0, 0), (1, 1), (1, 1), (0, 0)))
        field = sweep(field, padded, rhs, coefs, diag)
    return field

def reference(probes, permeability, absorption, sensitivity, observe_weight):
    kpad = jnp.pad(permeability, ((1, 1), (1, 1), (0, 0)))
    coefs, diag = face_terms(kpad, absorption)

    def respond(block):
        forward = jacobi(sensitivity * block.astype(jnp.float32), coefs, diag)
        adjoint = jacobi(observe_weight * forward, coefs, diag)
        return sensitivity * adjoint
    groups = probes.reshape(PROBES // 8, 8, NX, NY, NZ)
    responses = lax.map(respond, groups).reshape(PROBES, NX * NY * NZ)
    gram = jnp.dot(responses.astype(jnp.float32), responses.T.astype(jnp.float32), precision=lax.Precision.HIGHEST, preferred_element_type=jnp.float32) / float(NX * NY * NZ)
    r_factor = jnp.linalg.cholesky(gram).T
    q_basis = lax.linalg.triangular_solve(r_factor, responses, left_side=True, lower=False, transpose_a=True)
    return (q_basis.reshape(PROBES, NX, NY, NZ), r_factor)
```

```python
import functools

import jax
import jax.numpy as jnp
from jax import lax
from jax.experimental import pallas as pl
from jax.experimental.pallas import tpu as pltpu
from jax.sharding import PartitionSpec as P

OMEGA = 0.8
KEEP = 1.0 - OMEGA
A0 = 1.0 + KEEP + KEEP**2 + KEEP**3
A1 = 1.0 + 2.0 * KEEP + 3.0 * KEEP**2
A2 = 1.0 + 3.0 * KEEP
A3 = 1.0
DEPTH = 6
HALF = 32
GROUPS = (1, 1, 1, 1)
MIB = 1 << 20


def smem():
    return pl.BlockSpec(memory_space=pltpu.SMEM)


def vmem():
    return pl.BlockSpec(memory_space=pltpu.VMEM)


def prep_kernel(h_ref, mine_ref, theirs_ref, own_ref, send_ref, edge_ref, wide):
    planes, rows = mine_ref.shape[1], mine_ref.shape[2]
    side = h_ref[0]
    for source, target in ((theirs_ref, send_ref), (mine_ref, own_ref)):
        wide[...] = source[...].astype(jnp.float32).reshape(wide.shape)

        def plane(x, carry):
            for y in range(rows):
                target[x, y] = wide[pl.ds(x * rows + y, 8, stride=planes * rows), :]
            return carry

        lax.fori_loop(0, planes, plane, 0)
    edge_ref[...] = own_ref[pl.ds(side * (planes - DEPTH), DEPTH)]


def prep(side, probes, tile):
    planes, rows, depth = probes.shape[1:]
    block = (8, planes, rows, depth)
    per_half = HALF // 8
    whole = jax.ShapeDtypeStruct((planes, rows, 8, depth), jnp.float32)
    edge = jax.ShapeDtypeStruct((DEPTH, rows, 8, depth), jnp.float32)
    return pl.pallas_call(
        prep_kernel,
        grid_spec=pltpu.PrefetchScalarGridSpec(
            num_scalar_prefetch=1,
            grid=(1,),
            in_specs=[
                pl.BlockSpec(block, lambda i, h: (h[0] * per_half + tile, 0, 0, 0)),
                pl.BlockSpec(block, lambda i, h: ((1 - h[0]) * per_half + tile, 0, 0, 0)),
            ],
            out_specs=[
                pl.BlockSpec(whole.shape, lambda i, h: (0, 0, 0, 0)),
                pl.BlockSpec(whole.shape, lambda i, h: (0, 0, 0, 0)),
                pl.BlockSpec(edge.shape, lambda i, h: (0, 0, 0, 0)),
            ],
            scratch_shapes=[pltpu.VMEM((8 * planes * rows, depth), jnp.float32)],
        ),
        out_shape=[whole, whole, edge],
        compiler_params=pltpu.CompilerParams(vmem_limit_bytes=12 * MIB),
        cost_estimate=pl.CostEstimate(flops=0, bytes_accessed=2 * MIB, transcendentals=0),
        name="spread_probes",
    )(side, probes, probes)


def solve_kernel(h_ref, coef, own, recv, e1, e2, ylo, yhi, keep, back, r_s, a_s, b_s):
    planes, rows = own.shape[0], own.shape[1]
    wide_x, wide_y = r_s.shape[0], r_s.shape[1]
    side = h_ref[0]
    top = DEPTH + 2 * planes
    parts = (
        (own, 0, planes, DEPTH + planes * side),
        (recv, planes, planes, DEPTH + planes * (1 - side)),
        (e1, 2 * planes, DEPTH, top * (1 - side)),
        (e2, 2 * planes + DEPTH, DEPTH, top * side),
    )

    def row(which, x, y):
        return coef[which, x, pl.ds(y, 1), :]

    for piece, role, count, place in parts:

        def fill(i, carry, piece=piece, role=role, place=place):
            x = place + i
            for y in range(wide_y):
                if y < DEPTH:
                    value = ylo[role + i, y]
                elif y < DEPTH + rows:
                    value = piece[i, y - DEPTH]
                else:
                    value = yhi[role + i, y - DEPTH - rows]
                r_s[x, y] = value * row(6, x, y)
            return carry

        lax.fori_loop(0, count, fill, 0)

    def stencil(src, r, x, y, scale):
        here = src[x, y]
        total = row(0, x, y) * src[x - 1, y] + row(1, x, y) * src[x + 1, y]
        total = total + row(2, x, y) * src[x, y - 1] + row(3, x, y) * src[x, y + 1]
        total = total + row(4, x, y) * pltpu.roll(here, 1, 1) + row(5, x, y) * pltpu.roll(here, 127, 1)
        return r[x, y] + scale * total

    def sweep(src, dst, r, low, scale, last=None):
        def plane(x, carry):
            for y in range(low, wide_y - low):
                value = stencil(src, r, x, y, scale)
                if last is not None:
                    value = value * row(last, x, y)
                dst[x, y] = value
            return carry

        lax.fori_loop(low, wide_x - low, plane, 0)

    sweep(r_s, a_s, r_s, 1, A3 / A2)
    sweep(a_s, b_s, r_s, 2, A2 / A1)
    sweep(b_s, a_s, r_s, 3, A1 / A0, last=7)
    sweep(a_s, b_s, a_s, 4, A3 / A2)
    sweep(b_s, r_s, a_s, 5, A2 / A1)
    for target, place in ((back, parts[1][3]), (keep, parts[0][3])):

        def out(i, carry, target=target, place=place):
            x = place + i
            for y in range(rows):
                target[i, y] = stencil(r_s, a_s, x, y + DEPTH, A1 / A0) * row(8, x, y + DEPTH)
            return carry

        lax.fori_loop(0, planes, out, 0)


def solve(side, coef, own, recv, e1, e2, ylo, yhi):
    wide_x, wide_y = coef.shape[1], coef.shape[2]
    many, depth = own.shape[2:]
    field = pltpu.VMEM((wide_x, wide_y, many, depth), jnp.float32)
    cells = wide_x * wide_y * many * depth
    return pl.pallas_call(
        solve_kernel,
        in_specs=[smem()] + [vmem()] * 7,
        out_specs=[vmem(), vmem()],
        out_shape=[jax.ShapeDtypeStruct(own.shape, jnp.float32)] * 2,
        scratch_shapes=[field, field, field],
        compiler_params=pltpu.CompilerParams(vmem_limit_bytes=(14 + 14 * many // 8) * MIB),
        cost_estimate=pl.CostEstimate(flops=60 * cells, bytes_accessed=12 * MIB, transcendentals=0),
        name="both_solves",
    )(side, coef, own, recv, e1, e2, ylo, yhi)


def stacked(tiles, rows):
    return jnp.concatenate(
        [jnp.concatenate([t[0, y] for t in tiles], axis=0) for y in range(rows)], axis=1
    )


def split(value):
    high = value.astype(jnp.bfloat16)
    return high, (value - high.astype(jnp.float32)).astype(jnp.bfloat16)


def gram_kernel(scale, h_ref, *refs):
    tiles, out, total = refs[:-2], refs[-2], refs[-1]
    step = pl.program_id(0)

    @pl.when(step == 0)
    def _():
        total[...] = jnp.zeros_like(total)

    both = jnp.concatenate(split(stacked(tiles, tiles[0].shape[1])), axis=0)
    total[...] += lax.dot_general(both, both, (((1,), (1,)), ((), ())), preferred_element_type=jnp.float32)

    @pl.when(step == pl.num_programs(0) - 1)
    def _():
        n = out.shape[0]
        g = total[:n, :n] + total[:n, n:] + total[n:, :n] + total[n:, n:]
        half = n // 2
        turned = jnp.concatenate([g[half:], g[:half]], axis=0)
        turned = jnp.concatenate([turned[:, half:], turned[:, :half]], axis=1)
        out[...] = jnp.where(h_ref[0] == 0, g, turned) * scale


def tile_spec(shape):
    return pl.BlockSpec((1,) + shape[1:], lambda i: (i, 0, 0, 0))


def gram_of(side, tiles, cells):
    count = 8 * len(tiles)
    return pl.pallas_call(
        functools.partial(gram_kernel, 1.0 / cells),
        grid=(tiles[0].shape[0],),
        in_specs=[smem()] + [tile_spec(t.shape) for t in tiles],
        out_specs=pl.BlockSpec((count, count), lambda i: (0, 0)),
        out_shape=jax.ShapeDtypeStruct((count, count), jnp.float32),
        scratch_shapes=[pltpu.VMEM((2 * count, 2 * count), jnp.float32)],
        compiler_params=pltpu.CompilerParams(vmem_limit_bytes=16 * MIB),
        cost_estimate=pl.CostEstimate(flops=0, bytes_accessed=6 * MIB, transcendentals=0),
        name="gram",
    )(side, *tiles)


def factor(gram):
    n = gram.shape[0]
    unit = (lax.broadcasted_iota(jnp.int32, (n, n), 0) == lax.broadcasted_iota(jnp.int32, (n, n), 1)).astype(jnp.float32)
    both = jnp.concatenate([gram, unit], axis=1)
    rows = [both[8 * i : 8 * i + 8] for i in range(n // 8)]
    place = lax.broadcasted_iota(jnp.int32, (8, 2 * n), 0)
    for j in range(n):
        t, s = divmod(j, 8)
        pivot = rows[t][s : s + 1]
        pivot = pivot * lax.rsqrt(pivot[:, j : j + 1])
        lead = pivot[:, j : j + 1]
        for i in range(t, n // 8):
            new = rows[i] - (rows[i][:, j : j + 1] / lead) * pivot
            if i == t:
                new = jnp.where(place > s, new, jnp.where(place == s, pivot, rows[i]))
            rows[i] = new
    done = jnp.concatenate(rows, axis=0)
    return done[:, :n], done[:, n:]


def basis_kernel(h_ref, a_ref, b_ref, *refs):
    tiles, (q_ref, r_ref, left) = refs[:-3], refs[-3:]
    n = r_ref.shape[0]
    rows = tiles[0].shape[1]

    @pl.when(pl.program_id(0) == 0)
    def _():
        upper, inverse = factor(a_ref[...] + b_ref[...])
        i = lax.broadcasted_iota(jnp.int32, (n, n), 0)
        j = lax.broadcasted_iota(jnp.int32, (n, n), 1)
        r_ref[...] = jnp.where(j >= i, upper, 0.0)
        inverse = jnp.where(j <= i, inverse, 0.0)
        turned = jnp.concatenate([inverse[:, n // 2 :], inverse[:, : n // 2]], axis=1)
        high, low = split(jnp.where(h_ref[0] == 0, inverse, turned))
        left[...] = jnp.concatenate([high, high, low, low], axis=1)

    high, low = split(stacked(tiles, rows))
    q = jnp.dot(left[...], jnp.concatenate([high, low, high, low], axis=0), preferred_element_type=jnp.float32)
    depth = q.shape[1] // rows
    flat = q_ref.reshape(n * rows, depth)
    for y in range(rows):
        flat[pl.ds(y, n, stride=rows), :] = q[:, y * depth : (y + 1) * depth]


def basis(side, a, b, tiles):
    n = a.shape[0]
    planes, rows, _, depth = tiles[0].shape
    full = pl.BlockSpec((n, n), lambda i: (0, 0))
    return pl.pallas_call(
        basis_kernel,
        grid=(planes,),
        in_specs=[smem(), full, full] + [tile_spec(t.shape) for t in tiles],
        out_specs=[pl.BlockSpec((n, 1, rows, depth), lambda i: (0, i, 0, 0)), full],
        out_shape=[
            jax.ShapeDtypeStruct((n, planes, rows, depth), jnp.float32),
            jax.ShapeDtypeStruct((n, n), jnp.float32),
        ],
        scratch_shapes=[pltpu.VMEM((n, 4 * n), jnp.bfloat16)],
        compiler_params=pltpu.CompilerParams(vmem_limit_bytes=24 * MIB),
        cost_estimate=pl.CostEstimate(flops=0, bytes_accessed=8 * MIB, transcendentals=0),
        name="basis",
    )(side, a, b, *tiles)


def swap(value):
    return lax.ppermute(value, "gx", [(i, i ^ 1) for i in range(lax.axis_size("gx"))])


def outward(value):
    n = lax.axis_size("gx")
    return lax.ppermute(value, "gx", [(i, i + 2 * (i % 2) * 2 - 2) for i in range(n) if 0 <= i + 4 * (i % 2) - 2 < n])


def inward(value):
    n = lax.axis_size("gx")
    return lax.ppermute(value, "gx", [(i, i + 2 - 4 * (i % 2)) for i in range(n) if 0 <= i + 2 - 4 * (i % 2) < n])


def above(value):
    n = lax.axis_size("gy")
    return lax.ppermute(value, "gy", [(i, i + 1) for i in range(n - 1)])


def below(value):
    n = lax.axis_size("gy")
    return lax.ppermute(value, "gy", [(i + 1, i) for i in range(n - 1)])


def summed(value):
    steps = []
    for axis in ("gy", "gx"):
        n = lax.axis_size(axis)
        assert n & (n - 1) == 0
        shift = 1
        while shift < n:
            steps.append((axis, shift, n))
            shift *= 2
    other = None
    for axis, shift, n in steps:
        if other is not None:
            value = value + other
        other = lax.ppermute(value, axis, [(i, i ^ shift) for i in range(n)])
    return value, other


def coefficients(side, permeability, absorption, sensitivity, observe_weight):
    planes, rows, depth = permeability.shape
    lower = side == 0
    ring = DEPTH + 1
    own = jnp.stack([permeability, absorption, sensitivity, observe_weight])
    recv = swap(own)
    e1 = outward(jnp.where(lower, own[:, :ring], own[:, planes - ring :]))
    e2 = inward(jnp.where(lower, recv[:, planes - ring :], recv[:, :ring]))
    tall = jnp.concatenate(
        [
            jnp.where(lower, e2, e1),
            jnp.where(lower, own, recv),
            jnp.where(lower, recv, own),
            jnp.where(lower, e1, e2),
        ],
        axis=1,
    )
    low = above(tall[:, :, rows - ring :])
    high = below(tall[:, :, :ring])
    k, absorb, sense, weight = jnp.concatenate([low, tall, high], axis=2)

    def shifted(dx, dy):
        return k[1 + dx : k.shape[0] - 1 + dx, 1 + dy : k.shape[1] - 1 + dy]

    mid = shifted(0, 0)
    faces = [0.5 * (mid + shifted(*d)) for d in ((-1, 0), (1, 0), (0, -1), (0, 1))]
    zpad = jnp.pad(mid, ((0, 0), (0, 0), (1, 1)))
    z_low = 0.5 * (mid + zpad[:, :, :-2])
    z_high = 0.5 * (mid + zpad[:, :, 2:])
    diag = absorb[1:-1, 1:-1] + sum(faces) + z_low + z_high

    def inside(axis, length, start, total):
        index = start - DEPTH + lax.broadcasted_iota(jnp.int32, diag.shape, axis)
        return (index >= 0) & (index < total)

    gx, gy = lax.axis_index("gx"), lax.axis_index("gy")
    here = inside(0, planes, (gx - side) * planes, planes * lax.axis_size("gx"))
    here = here & inside(1, rows, gy * rows, rows * lax.axis_size("gy"))
    inv = jnp.where(here, OMEGA / jnp.where(here, diag, 1.0), 0.0)
    z = lax.broadcasted_iota(jnp.int32, diag.shape, 2)
    z_low = jnp.where(z == 0, 0.0, z_low)
    z_high = jnp.where(z == depth - 1, 0.0, z_high)
    sense, weight = sense[1:-1, 1:-1], weight[1:-1, 1:-1]
    return jnp.stack([f * inv for f in faces] + [z_low * inv, z_high * inv, sense * inv, A0 * weight * inv, A0 * sense])


def body(probes, permeability, absorption, sensitivity, observe_weight):
    count, planes, rows, depth = probes.shape
    cells = planes * lax.axis_size("gx") * rows * lax.axis_size("gy") * depth
    side = lax.axis_index("gx") % 2
    flag = side.reshape(1).astype(jnp.int32)
    coef = coefficients(side, permeability, absorption, sensitivity, observe_weight)

    keeps, gots = [], []
    tile = 0
    for many in GROUPS:
        pieces = [prep(flag, probes, tile + i) for i in range(many)]
        tile += many
        own, send, edge = (jnp.concatenate(p, axis=2) if many > 1 else p[0] for p in zip(*pieces))
        recv = swap(send)
        e1 = outward(edge)
        e2 = inward(lax.dynamic_slice_in_dim(recv, (1 - side) * (planes - DEPTH), DEPTH, 0))
        ends = [(p[:, :DEPTH], p[:, rows - DEPTH :]) for p in (own, recv, e1, e2)]
        yhi = below(jnp.concatenate([first for first, _ in ends], axis=0))
        ylo = above(jnp.concatenate([last for _, last in ends], axis=0))
        keep, back = solve(flag, coef, own, recv, e1, e2, ylo, yhi)
        got = swap(back)
        for i in range(many):
            keeps.append(keep[:, :, 8 * i : 8 * i + 8] if many > 1 else keep)
            gots.append(got[:, :, 8 * i : 8 * i + 8] if many > 1 else got)
    tiles = keeps + gots
    a, b = summed(gram_of(flag, tiles, cells))
    q, r = basis(flag, a, b, tiles)
    return (q, r)


def solution(mesh):
    return jax.shard_map(
        body,
        mesh=mesh,
        in_specs=(
            P(None, "gx", "gy", None),
            P("gx", "gy", None),
            P("gx", "gy", None),
            P("gx", "gy", None),
            P("gx", "gy", None),
        ),
        out_specs=(P(None, "gx", "gy", None), P()),
        check_vma=False,
    )
```

```python
import functools

import jax
import jax.numpy as jnp
from jax import lax
from jax.experimental import pallas as pl
from jax.experimental.pallas import tpu as pltpu
from jax.sharding import PartitionSpec as P

OMEGA = 0.8
KEEP = 1.0 - OMEGA
A0 = 1.0 + KEEP + KEEP**2 + KEEP**3
A1 = 1.0 + 2.0 * KEEP + 3.0 * KEEP**2
A2 = 1.0 + 3.0 * KEEP
A3 = 1.0
DEPTH = 6
RING = DEPTH + 1
EDGE = 8
MIB = 1 << 20


def smem():
    return pl.BlockSpec(memory_space=pltpu.SMEM)


def vmem():
    return pl.BlockSpec(memory_space=pltpu.VMEM)


def prep_kernel(h_ref, mine_ref, theirs_ref, *refs):
    maps, (own_ref, send_ref, edge_ref, wide) = refs[:-4], refs[-4:]
    planes, rows, many, depth = own_ref.shape
    side = h_ref[0]
    cells = planes * rows
    send = send_ref.at[pl.ds(0, cells * many)].reshape(own_ref.shape)
    for source, target in ((theirs_ref, send), (mine_ref, own_ref)):
        wide[...] = source[...].astype(jnp.float32).reshape(wide.shape)

        def plane(x, carry):
            for y in range(rows):
                target[x, y] = wide[pl.ds(x * rows + y, many, stride=cells), :]
            return carry

        lax.fori_loop(0, planes, plane, 0)
    edge = DEPTH * rows * many
    edge_ref[:edge] = own_ref[pl.ds(side * (planes - DEPTH), DEPTH)].reshape(edge, depth)
    for i, ref in enumerate(maps):
        at, ring = cells * many + i * cells, RING * rows
        send_ref[at : at + cells] = ref[...].reshape(cells, depth)
        part = ref[pl.ds(side * (planes - RING), RING)].reshape(ring, depth)
        edge_ref[edge + i * ring : edge + (i + 1) * ring] = part


def prep(side, probes, tile, maps):
    planes, rows, depth = probes.shape[1:]
    block = (8, planes, rows, depth)
    own = (planes, rows, 8, depth)
    send = (planes * rows * (8 + len(maps)), depth)
    edge = ((DEPTH * 8 + RING * len(maps)) * rows, depth)
    return pl.pallas_call(
        prep_kernel,
        grid_spec=pltpu.PrefetchScalarGridSpec(
            num_scalar_prefetch=1,
            grid=(1,),
            in_specs=[
                pl.BlockSpec(block, lambda i, h: (2 * tile + h[0], 0, 0, 0)),
                pl.BlockSpec(block, lambda i, h: (2 * tile + 1 - h[0], 0, 0, 0)),
            ]
            + [pl.BlockSpec(m.shape, lambda i, h: (0, 0, 0)) for m in maps],
            out_specs=[
                pl.BlockSpec(own, lambda i, h: (0, 0, 0, 0)),
                pl.BlockSpec(send, lambda i, h: (0, 0)),
                pl.BlockSpec(edge, lambda i, h: (0, 0)),
            ],
            scratch_shapes=[pltpu.VMEM((8 * planes * rows, depth), jnp.float32)],
        ),
        out_shape=[jax.ShapeDtypeStruct(s, jnp.float32) for s in (own, send, edge)],
        compiler_params=pltpu.CompilerParams(vmem_limit_bytes=16 * MIB),
        cost_estimate=pl.CostEstimate(flops=0, bytes_accessed=2 * MIB, transcendentals=0),
        name="spread_probes",
    )(side, probes, probes, *maps)


def spread(coef, which, x, y, many):
    return coef[which, x, pl.ds(y, many, stride=0), :]


def solve_kernel(h_ref, coef, own, recv, e1, e2, ylo, yhi, keep, back, r_s, a_s, b_s):
    planes, rows = own.shape[0], own.shape[1]
    wide_x, wide_y = r_s.shape[0], r_s.shape[1]
    side = h_ref[0]
    top = DEPTH + 2 * planes
    parts = (
        (own, 0, planes, DEPTH + planes * side),
        (recv, planes, planes, DEPTH + planes * (1 - side)),
        (e1, 2 * planes, DEPTH, top * (1 - side)),
        (e2, 2 * planes + DEPTH, DEPTH, top * side),
    )

    def row(which, x, y):
        return spread(coef, which, x, y, own.shape[2])

    for piece, role, count, place in parts:

        def fill(i, carry, piece=piece, role=role, place=place):
            x = place + i
            for y in range(wide_y):
                if y < DEPTH:
                    value = ylo[role + i, y]
                elif y < DEPTH + rows:
                    value = piece[i, y - DEPTH]
                else:
                    value = yhi[role + i, y - DEPTH - rows]
                r_s[x, y] = value * row(6, x, y)
            return carry

        lax.fori_loop(0, count, fill, 0)

    def stencil(src, r, x, low, scale):
        here = [src[x, y] for y in range(low - 1, wide_y - low + 1)]
        for y in range(low, wide_y - low):
            k = y - low + 1
            total = row(0, x, y) * src[x - 1, y] + row(1, x, y) * src[x + 1, y]
            total = total + row(2, x, y) * here[k - 1] + row(3, x, y) * here[k + 1]
            total = total + row(4, x, y) * pltpu.roll(here[k], 1, 1) + row(5, x, y) * pltpu.roll(here[k], 127, 1)
            yield y, r[x, y] + scale * total

    def sweep(src, dst, r, low, scale, last=None):
        def plane(x, carry):
            for y, value in stencil(src, r, x, low, scale):
                dst[x, y] = value if last is None else value * row(last, x, y)
            return carry

        lax.fori_loop(low, wide_x - low, plane, 0)

    sweep(r_s, a_s, r_s, 1, A3 / A2)
    sweep(a_s, b_s, r_s, 2, A2 / A1)
    sweep(b_s, a_s, r_s, 3, A1 / A0, last=7)
    sweep(a_s, b_s, a_s, 4, A3 / A2)
    sweep(b_s, r_s, a_s, 5, A2 / A1)
    for target, place in ((back, parts[1][3]), (keep, parts[0][3])):

        def out(i, carry, target=target, place=place):
            x = place + i
            for y, value in stencil(r_s, a_s, x, DEPTH, A1 / A0):
                target[i, y - DEPTH] = value * row(8, x, y)
            return carry

        lax.fori_loop(0, planes, out, 0)


def solve(side, coef, own, recv, e1, e2, ylo, yhi):
    wide_x, wide_y = coef.shape[1], coef.shape[2]
    many, depth = own.shape[2:]
    field = pltpu.VMEM((wide_x, wide_y, many, depth), jnp.float32)
    cells = wide_x * wide_y * many * depth
    return pl.pallas_call(
        solve_kernel,
        in_specs=[smem()] + [vmem()] * 7,
        out_specs=[vmem(), vmem()],
        out_shape=[jax.ShapeDtypeStruct(own.shape, jnp.float32)] * 2,
        scratch_shapes=[field, field, field],
        compiler_params=pltpu.CompilerParams(vmem_limit_bytes=(14 + 14 * many // 8) * MIB),
        cost_estimate=pl.CostEstimate(flops=60 * cells, bytes_accessed=12 * MIB, transcendentals=0),
        name="both_solves",
    )(side, coef, own, recv, e1, e2, ylo, yhi)


def stacked(side, tiles, rows):
    columns = []
    for y in range(rows):
        parts = []
        for keep, got in zip(tiles[0::2], tiles[1::2]):
            a, b = keep[0, y], got[0, y]
            parts += [jnp.where(side == 0, a, b), jnp.where(side == 0, b, a)]
        columns.append(jnp.concatenate(parts, axis=0))
    return jnp.concatenate(columns, axis=1)


def split(value):
    high = value.astype(jnp.bfloat16)
    return high, (value - high.astype(jnp.float32)).astype(jnp.bfloat16)


def gram_kernel(scale, h_ref, *refs):
    tiles, out, total = refs[:-2], refs[-2], refs[-1]
    step = pl.program_id(0)

    @pl.when(step == 0)
    def _():
        total[...] = jnp.zeros_like(total)

    both = jnp.concatenate(split(stacked(h_ref[0], tiles, tiles[0].shape[1])), axis=0)
    total[...] += lax.dot_general(both, both, (((1,), (1,)), ((), ())), preferred_element_type=jnp.float32)

    @pl.when(step == pl.num_programs(0) - 1)
    def _():
        n = out.shape[0]
        g = total[:n, :n] + total[:n, n:] + total[n:, :n] + total[n:, n:]
        out[...] = g * scale


def tile_spec(shape):
    return pl.BlockSpec((1,) + shape[1:], lambda i: (i, 0, 0, 0))


def gram_of(side, tiles, cells):
    count = 8 * len(tiles)
    return pl.pallas_call(
        functools.partial(gram_kernel, 1.0 / cells),
        grid=(tiles[0].shape[0],),
        in_specs=[smem()] + [tile_spec(t.shape) for t in tiles],
        out_specs=pl.BlockSpec((count, count), lambda i: (0, 0)),
        out_shape=jax.ShapeDtypeStruct((count, count), jnp.float32),
        scratch_shapes=[pltpu.VMEM((2 * count, 2 * count), jnp.float32)],
        compiler_params=pltpu.CompilerParams(vmem_limit_bytes=16 * MIB),
        cost_estimate=pl.CostEstimate(flops=0, bytes_accessed=6 * MIB, transcendentals=0),
        name="gram",
    )(side, *tiles)


def factor(gram):
    n = gram.shape[0]
    i = lax.broadcasted_iota(jnp.int32, (n, n), 0)
    j = lax.broadcasted_iota(jnp.int32, (n, n), 1)
    both = jnp.concatenate([gram, (i == j).astype(jnp.float32)], axis=1)
    rows = [both[8 * t : 8 * t + 8] for t in range(n // 8)]
    place = lax.broadcasted_iota(jnp.int32, (8, 2 * n), 0)
    for c in range(0, n, 2):
        t, s = divmod(c, 8)
        first, second = rows[t][s : s + 1], rows[t][s + 1 : s + 2]
        a, b, d = first[:, c : c + 1], first[:, c + 1 : c + 2], second[:, c + 1 : c + 2]
        inv = 1.0 / (a * d - b * b)
        w1 = (d * first - b * second) * inv
        w2 = (a * second - b * first) * inv
        fixed = jnp.where(place == s + 1, second - (b / a) * first, rows[t])
        for k in range(t, n // 8):
            new = rows[k] - (rows[k][:, c : c + 1] * w1 + rows[k][:, c + 1 : c + 2] * w2)
            rows[k] = jnp.where(place > s + 1, new, fixed) if k == t else new
    done = jnp.concatenate(rows, axis=0)
    size = jnp.sum(jnp.where(i == j, done[:, :n], 0.0), axis=1, keepdims=True)
    done = done * lax.rsqrt(size)
    return done[:, :n], done[:, n:]


def basis_kernel(h_ref, a_ref, b_ref, *refs):
    tiles, (q_ref, r_ref, left) = refs[:-3], refs[-3:]
    n = r_ref.shape[0]
    rows = tiles[0].shape[1]

    @pl.when(pl.program_id(0) == 0)
    def _():
        upper, inverse = factor(a_ref[...] + b_ref[...])
        i = lax.broadcasted_iota(jnp.int32, (n, n), 0)
        j = lax.broadcasted_iota(jnp.int32, (n, n), 1)
        r_ref[...] = jnp.where(j >= i, upper, 0.0)
        inverse = jnp.where(j <= i, inverse, 0.0)
        high, low = split(inverse)
        left[...] = jnp.concatenate([high, high, low, low], axis=1)

    high, low = split(stacked(h_ref[0], tiles, rows))
    q = jnp.dot(left[...], jnp.concatenate([high, low, high, low], axis=0), preferred_element_type=jnp.float32)
    depth = q.shape[1] // rows
    flat = q_ref.reshape(n * rows, depth)
    for y in range(rows):
        flat[pl.ds(y, n, stride=rows), :] = q[:, y * depth : (y + 1) * depth]


def basis(side, a, b, tiles):
    n = a.shape[0]
    planes, rows, _, depth = tiles[0].shape
    full = pl.BlockSpec((n, n), lambda i: (0, 0))
    return pl.pallas_call(
        basis_kernel,
        grid=(planes,),
        in_specs=[smem(), full, full] + [tile_spec(t.shape) for t in tiles],
        out_specs=[pl.BlockSpec((n, 1, rows, depth), lambda i: (0, i, 0, 0)), full],
        out_shape=[
            jax.ShapeDtypeStruct((n, planes, rows, depth), jnp.float32),
            jax.ShapeDtypeStruct((n, n), jnp.float32),
        ],
        scratch_shapes=[pltpu.VMEM((n, 4 * n), jnp.bfloat16)],
        compiler_params=pltpu.CompilerParams(vmem_limit_bytes=24 * MIB),
        cost_estimate=pl.CostEstimate(flops=0, bytes_accessed=8 * MIB, transcendentals=0),
        name="basis",
    )(side, a, b, *tiles)


def swap(value):
    return lax.ppermute(value, "gx", [(i, i ^ 1) for i in range(lax.axis_size("gx"))])


def outward(value):
    n = lax.axis_size("gx")
    return lax.ppermute(value, "gx", [(i, i + 2 * (i % 2) * 2 - 2) for i in range(n) if 0 <= i + 4 * (i % 2) - 2 < n])


def inward(value):
    n = lax.axis_size("gx")
    return lax.ppermute(value, "gx", [(i, i + 2 - 4 * (i % 2)) for i in range(n) if 0 <= i + 2 - 4 * (i % 2) < n])


def above(value):
    n = lax.axis_size("gy")
    return lax.ppermute(value, "gy", [(i, i + 1) for i in range(n - 1)])


def below(value):
    n = lax.axis_size("gy")
    return lax.ppermute(value, "gy", [(i + 1, i) for i in range(n - 1)])


def summed(value):
    steps = []
    for axis in ("gy", "gx"):
        n = lax.axis_size(axis)
        assert n & (n - 1) == 0
        shift = 1
        while shift < n:
            steps.append((axis, shift, n))
            shift *= 2
    other = None
    for axis, shift, n in steps:
        if other is not None:
            value = value + other
        other = lax.ppermute(value, axis, [(i, i ^ shift) for i in range(n)])
    return value, other


def coefficients(side, ext, planes, rows):
    cut = EDGE - DEPTH
    k, absorb, sense, weight = ext
    depth = k.shape[2]

    def shifted(value, dx, dy):
        return value[1 + dx : value.shape[0] - 1 + dx, cut + dy : value.shape[1] - cut + dy]

    mid = shifted(k, 0, 0)
    faces = [0.5 * (mid + shifted(k, *d)) for d in ((-1, 0), (1, 0), (0, -1), (0, 1))]
    zpad = jnp.pad(mid, ((0, 0), (0, 0), (1, 1)))
    z_low = 0.5 * (mid + zpad[:, :, :-2])
    z_high = 0.5 * (mid + zpad[:, :, 2:])
    diag = shifted(absorb, 0, 0) + sum(faces) + z_low + z_high

    def inside(axis, start, total):
        index = start - DEPTH + lax.broadcasted_iota(jnp.int32, diag.shape, axis)
        return (index >= 0) & (index < total)

    gx, gy = lax.axis_index("gx"), lax.axis_index("gy")
    here = inside(0, (gx - side) * planes, planes * lax.axis_size("gx"))
    here = here & inside(1, gy * rows, rows * lax.axis_size("gy"))
    inv = jnp.where(here, OMEGA / jnp.where(here, diag, 1.0), 0.0)
    z = lax.broadcasted_iota(jnp.int32, diag.shape, 2)
    z_low = jnp.where(z == 0, 0.0, z_low)
    z_high = jnp.where(z == depth - 1, 0.0, z_high)
    sense, weight = shifted(sense, 0, 0), shifted(weight, 0, 0)
    return jnp.stack([f * inv for f in faces] + [z_low * inv, z_high * inv, sense * inv, A0 * weight * inv, A0 * sense])


def rows_of(*values):
    parts = [v.reshape(-1, v.shape[-1]) for v in values]
    return parts[0] if len(parts) == 1 else jnp.concatenate(parts, axis=0)


def parts_of(flat, *shapes):
    out, at = [], 0
    for shape in shapes:
        size = 1
        for n in shape[:-1]:
            size *= n
        out.append(flat[at : at + size].reshape(shape))
        at += size
    return out


def body(probes, permeability, absorption, sensitivity, observe_weight):
    count, planes, rows, depth = probes.shape
    cells = planes * lax.axis_size("gx") * rows * lax.axis_size("gy") * depth
    side = lax.axis_index("gx") % 2
    lower = side == 0
    flag = side.reshape(1).astype(jnp.int32)
    maps = (permeability, absorption, sensitivity, observe_weight)
    tall = 2 * planes + 2 * DEPTH

    tiles = []
    coef = turn = None
    for tile in range(count // 16):
        mine = maps if tile == 0 else ()
        own, send, edge = prep(flag, probes, tile, mine)
        if turn is not None:
            send, turn = lax.optimization_barrier((send, turn))
        recv_rows = swap(send)
        e1_rows = outward(edge)
        block, halo = (planes, rows, 8, depth), (DEPTH, rows, 8, depth)
        four, ring = (len(maps), planes, rows, depth), (len(maps), RING, rows, depth)
        recv, *recv_maps = parts_of(recv_rows, block, *([four] if mine else []))
        inner = [lax.dynamic_slice_in_dim(recv, (1 - side) * (planes - DEPTH), DEPTH, 0)]
        for value in recv_maps:
            inner.append(lax.dynamic_slice_in_dim(value, (1 - side) * (planes - RING), RING, 1))
        e2_rows = inward(rows_of(*inner))
        e1, *e1_maps = parts_of(e1_rows, halo, *([ring] if mine else []))
        e2, *e2_maps = parts_of(e2_rows, halo, *([ring] if mine else []))
        turn = e1
        low = [jnp.concatenate([p[:, rows - DEPTH :] for p in (own, recv, e1, e2)], axis=0)]
        high = [jnp.concatenate([p[:, :DEPTH] for p in (own, recv, e1, e2)], axis=0)]
        if mine:
            own_maps = jnp.stack(maps)
            wide = jnp.concatenate(
                [
                    jnp.where(lower, e2_maps[0], e1_maps[0]),
                    jnp.where(lower, own_maps, recv_maps[0]),
                    jnp.where(lower, recv_maps[0], own_maps),
                    jnp.where(lower, e1_maps[0], e2_maps[0]),
                ],
                axis=1,
            )
            low.append(wide[:, :, rows - EDGE :])
            high.append(wide[:, :, :EDGE])
        shapes = [v.shape for v in low]
        ylo, *map_low = parts_of(above(rows_of(*low)), *shapes)
        yhi, *map_high = parts_of(below(rows_of(*high)), *shapes)
        if mine:
            coef = coefficients(side, jnp.concatenate([map_low[0], wide, map_high[0]], axis=2), planes, rows)
        keep, back = solve(flag, coef, own, recv, e1, e2, ylo, yhi)
        tiles += [keep, swap(back)]
    a, b = summed(gram_of(flag, tiles, cells))
    q, r = basis(flag, a, b, tiles)
    return (q, r)


def solution(mesh):
    return jax.shard_map(
        body,
        mesh=mesh,
        in_specs=(
            P(None, "gx", "gy", None),
            P("gx", "gy", None),
            P("gx", "gy", None),
            P("gx", "gy", None),
            P("gx", "gy", None),
        ),
        out_specs=(P(None, "gx", "gy", None), P()),
        check_vma=False,
    )
```

```python
import functools

import jax
import jax.numpy as jnp
from jax import lax
from jax.experimental import pallas as pl
from jax.experimental.pallas import tpu as pltpu
from jax.sharding import PartitionSpec as P

OMEGA = 0.8
KEEP = 1.0 - OMEGA
A0 = 1.0 + KEEP + KEEP**2 + KEEP**3
A1 = 1.0 + 2.0 * KEEP + 3.0 * KEEP**2
A2 = 1.0 + 3.0 * KEEP
A3 = 1.0
DEPTH = 6
RING = DEPTH + 1
EDGE = 8
GROUPS = (2, 2)
MIB = 1 << 20


def smem():
    return pl.BlockSpec(memory_space=pltpu.SMEM)


def vmem():
    return pl.BlockSpec(memory_space=pltpu.VMEM)


def prep_kernel(h_ref, mine_ref, theirs_ref, *refs):
    maps, (own_ref, send_ref, edge_ref, wide) = refs[:-4], refs[-4:]
    planes, rows, many, depth = own_ref.shape
    side = h_ref[0]
    cells = planes * rows
    send = send_ref.at[pl.ds(0, cells * many)].reshape(own_ref.shape)
    for source, target in ((theirs_ref, send), (mine_ref, own_ref)):
        wide[...] = source[...].astype(jnp.float32).reshape(wide.shape)

        def plane(x, carry):
            for y in range(rows):
                target[x, y] = wide[pl.ds(x * rows + y, many, stride=cells), :]
            return carry

        lax.fori_loop(0, planes, plane, 0)
    edge = DEPTH * rows * many
    edge_ref[:edge] = own_ref[pl.ds(side * (planes - DEPTH), DEPTH)].reshape(edge, depth)
    for i, ref in enumerate(maps):
        at, ring = cells * many + i * cells, RING * rows
        send_ref[at : at + cells] = ref[...].reshape(cells, depth)
        part = ref[pl.ds(side * (planes - RING), RING)].reshape(ring, depth)
        edge_ref[edge + i * ring : edge + (i + 1) * ring] = part


def prep(side, probes, tile, maps):
    planes, rows, depth = probes.shape[1:]
    block = (8, planes, rows, depth)
    own = (planes, rows, 8, depth)
    send = (planes * rows * (8 + len(maps)), depth)
    edge = ((DEPTH * 8 + RING * len(maps)) * rows, depth)
    return pl.pallas_call(
        prep_kernel,
        grid_spec=pltpu.PrefetchScalarGridSpec(
            num_scalar_prefetch=1,
            grid=(1,),
            in_specs=[
                pl.BlockSpec(block, lambda i, h: (2 * tile + h[0], 0, 0, 0)),
                pl.BlockSpec(block, lambda i, h: (2 * tile + 1 - h[0], 0, 0, 0)),
            ]
            + [pl.BlockSpec(m.shape, lambda i, h: (0, 0, 0)) for m in maps],
            out_specs=[
                pl.BlockSpec(own, lambda i, h: (0, 0, 0, 0)),
                pl.BlockSpec(send, lambda i, h: (0, 0)),
                pl.BlockSpec(edge, lambda i, h: (0, 0)),
            ],
            scratch_shapes=[pltpu.VMEM((8 * planes * rows, depth), jnp.float32)],
        ),
        out_shape=[jax.ShapeDtypeStruct(s, jnp.float32) for s in (own, send, edge)],
        compiler_params=pltpu.CompilerParams(vmem_limit_bytes=16 * MIB),
        cost_estimate=pl.CostEstimate(flops=0, bytes_accessed=2 * MIB, transcendentals=0),
        name="spread_probes",
    )(side, probes, probes, *maps)


def spread(coef, which, x, y, many):
    return coef[which, x, pl.ds(y, many, stride=0), :]


def solve_kernel(h_ref, coef, own, recv, e1, e2, ylo, yhi, keep, back, r_s, a_s, b_s):
    tiles, planes, rows, many, depth = own.shape
    wide_x, wide_y = r_s.shape[1], r_s.shape[2]
    side = h_ref[0]
    top = DEPTH + 2 * planes

    def fields(ref, n, m):
        return ref.at[pl.ds(0, tiles * n * m * many)].reshape(tiles, n, m, many, depth)

    ylo, yhi = fields(ylo, wide_x, DEPTH), fields(yhi, wide_x, DEPTH)
    parts = (
        (own, 0, planes, DEPTH + planes * side),
        (fields(recv, planes, rows), planes, planes, DEPTH + planes * (1 - side)),
        (fields(e1, DEPTH, rows), 2 * planes, DEPTH, top * (1 - side)),
        (fields(e2, DEPTH, rows), 2 * planes + DEPTH, DEPTH, top * side),
    )

    def row(which, x, y):
        return spread(coef, which, x, y, many)

    for piece, role, count, place in parts:

        def fill(i, carry, piece=piece, role=role, place=place):
            x = place + i
            for y in range(wide_y):
                scale = row(6, x, y)
                for t in range(tiles):
                    if y < DEPTH:
                        value = ylo[t, role + i, y]
                    elif y < DEPTH + rows:
                        value = piece[t, i, y - DEPTH]
                    else:
                        value = yhi[t, role + i, y - DEPTH - rows]
                    r_s[t, x, y] = value * scale
            return carry

        lax.fori_loop(0, count, fill, 0)

    def stencil(src, r, x, low, scale, last=None):
        span = range(tiles)
        prev = [src[t, x, low - 1] for t in span]
        here = [src[t, x, low] for t in span]
        for y in range(low, wide_y - low):
            after = [src[t, x, y + 1] for t in span]
            c = [row(k, x, y) for k in range(6)]
            end = None if last is None else row(last, x, y)
            values = []
            for t in span:
                total = c[0] * src[t, x - 1, y] + c[1] * src[t, x + 1, y]
                total = total + (c[2] * prev[t] + c[3] * after[t])
                total = total + (c[4] * pltpu.roll(here[t], 1, 1) + c[5] * pltpu.roll(here[t], 127, 1))
                value = r[t, x, y] + scale * total
                values.append(value if end is None else value * end)
            yield y, values
            prev, here = here, after

    def sweep(src, dst, r, low, scale, last=None):
        def plane(x, carry):
            for y, values in stencil(src, r, x, low, scale, last):
                for t, value in enumerate(values):
                    dst[t, x, y] = value
            return carry

        lax.fori_loop(low, wide_x - low, plane, 0)

    sweep(r_s, a_s, r_s, 1, A3 / A2)
    sweep(a_s, b_s, r_s, 2, A2 / A1)
    sweep(b_s, a_s, r_s, 3, A1 / A0, last=7)
    sweep(a_s, b_s, a_s, 4, A3 / A2)
    sweep(b_s, r_s, a_s, 5, A2 / A1)
    for target, place in ((back, parts[1][3]), (keep, parts[0][3])):

        def out(i, carry, target=target, place=place):
            for y, values in stencil(r_s, a_s, place + i, DEPTH, A1 / A0, last=8):
                for t, value in enumerate(values):
                    target[t, i, y - DEPTH] = value
            return carry

        lax.fori_loop(0, planes, out, 0)


def solve(side, coef, own, *messages):
    tiles, _, _, many, depth = own.shape
    wide_x, wide_y = coef.shape[1:3]
    field = pltpu.VMEM((tiles, wide_x, wide_y, many, depth), jnp.float32)
    cells = tiles * wide_x * wide_y * many * depth
    return pl.pallas_call(
        solve_kernel,
        in_specs=[smem()] + [vmem()] * 7,
        out_specs=[vmem(), vmem()],
        out_shape=[jax.ShapeDtypeStruct(own.shape, jnp.float32)] * 2,
        scratch_shapes=[field, field, field],
        compiler_params=pltpu.CompilerParams(vmem_limit_bytes=(14 + 14 * tiles) * MIB),
        cost_estimate=pl.CostEstimate(flops=60 * cells, bytes_accessed=12 * MIB, transcendentals=0),
        name="both_solves",
    )(side, coef, own, *messages)


def stacked(side, tiles, rows):
    columns = []
    for y in range(rows):
        parts = []
        for keep, got in zip(tiles[0::2], tiles[1::2]):
            a, b = keep[0, 0, y], got[0, 0, y]
            parts += [jnp.where(side == 0, a, b), jnp.where(side == 0, b, a)]
        columns.append(jnp.concatenate(parts, axis=0))
    return jnp.concatenate(columns, axis=1)


def split(value):
    high = value.astype(jnp.bfloat16)
    return high, (value - high.astype(jnp.float32)).astype(jnp.bfloat16)


def gram_kernel(scale, h_ref, *refs):
    tiles, out, total = refs[:-2], refs[-2], refs[-1]
    step = pl.program_id(0)

    @pl.when(step == 0)
    def _():
        total[...] = jnp.zeros_like(total)

    both = jnp.concatenate(split(stacked(h_ref[0], tiles, tiles[0].shape[2])), axis=0)
    total[...] += lax.dot_general(both, both, (((1,), (1,)), ((), ())), preferred_element_type=jnp.float32)

    @pl.when(step == pl.num_programs(0) - 1)
    def _():
        n = out.shape[0]
        g = total[:n, :n] + total[:n, n:] + total[n:, :n] + total[n:, n:]
        out[...] = g * scale


def tile_specs(groups):
    return [
        pl.BlockSpec((1, 1) + g.shape[2:], lambda i, t=t: (t, i, 0, 0, 0))
        for keep, got in groups
        for t in range(keep.shape[0])
        for g in (keep, got)
    ]


def tile_args(groups):
    return [g for keep, got in groups for t in range(keep.shape[0]) for g in (keep, got)]


def gram_of(side, groups, cells):
    tiles = tile_args(groups)
    count = 8 * len(tiles)
    return pl.pallas_call(
        functools.partial(gram_kernel, 1.0 / cells),
        grid=(tiles[0].shape[1],),
        in_specs=[smem()] + tile_specs(groups),
        out_specs=pl.BlockSpec((count, count), lambda i: (0, 0)),
        out_shape=jax.ShapeDtypeStruct((count, count), jnp.float32),
        scratch_shapes=[pltpu.VMEM((2 * count, 2 * count), jnp.float32)],
        compiler_params=pltpu.CompilerParams(vmem_limit_bytes=16 * MIB),
        cost_estimate=pl.CostEstimate(flops=0, bytes_accessed=6 * MIB, transcendentals=0),
        name="gram",
    )(side, *tiles)


def factor(gram):
    n = gram.shape[0]
    i = lax.broadcasted_iota(jnp.int32, (n, n), 0)
    j = lax.broadcasted_iota(jnp.int32, (n, n), 1)
    both = jnp.concatenate([gram, (i == j).astype(jnp.float32)], axis=1)
    rows = [both[8 * t : 8 * t + 8] for t in range(n // 8)]
    place = lax.broadcasted_iota(jnp.int32, (8, 2 * n), 0)
    for c in range(0, n, 2):
        t, s = divmod(c, 8)
        first, second = rows[t][s : s + 1], rows[t][s + 1 : s + 2]
        a, b, d = first[:, c : c + 1], first[:, c + 1 : c + 2], second[:, c + 1 : c + 2]
        inv = 1.0 / (a * d - b * b)
        w1 = (d * first - b * second) * inv
        w2 = (a * second - b * first) * inv
        fixed = jnp.where(place == s + 1, second - (b / a) * first, rows[t])
        for k in range(t, n // 8):
            new = rows[k] - (rows[k][:, c : c + 1] * w1 + rows[k][:, c + 1 : c + 2] * w2)
            rows[k] = jnp.where(place > s + 1, new, fixed) if k == t else new
    done = jnp.concatenate(rows, axis=0)
    size = jnp.sum(jnp.where(i == j, done[:, :n], 0.0), axis=1, keepdims=True)
    done = done * lax.rsqrt(size)
    return done[:, :n], done[:, n:]


def basis_kernel(h_ref, a_ref, b_ref, *refs):
    tiles, (q_ref, r_ref, left) = refs[:-3], refs[-3:]
    n = r_ref.shape[0]
    rows = tiles[0].shape[2]

    @pl.when(pl.program_id(0) == 0)
    def _():
        upper, inverse = factor(a_ref[...] + b_ref[...])
        i = lax.broadcasted_iota(jnp.int32, (n, n), 0)
        j = lax.broadcasted_iota(jnp.int32, (n, n), 1)
        r_ref[...] = jnp.where(j >= i, upper, 0.0)
        inverse = jnp.where(j <= i, inverse, 0.0)
        high, low = split(inverse)
        left[...] = jnp.concatenate([high, high, low, low], axis=1)

    high, low = split(stacked(h_ref[0], tiles, rows))
    q = jnp.dot(left[...], jnp.concatenate([high, low, high, low], axis=0), preferred_element_type=jnp.float32)
    depth = q.shape[1] // rows
    flat = q_ref.reshape(n * rows, depth)
    for y in range(rows):
        flat[pl.ds(y, n, stride=rows), :] = q[:, y * depth : (y + 1) * depth]


def basis(side, a, b, groups):
    n = a.shape[0]
    tiles = tile_args(groups)
    _, planes, rows, _, depth = tiles[0].shape
    full = pl.BlockSpec((n, n), lambda i: (0, 0))
    return pl.pallas_call(
        basis_kernel,
        grid=(planes,),
        in_specs=[smem(), full, full] + tile_specs(groups),
        out_specs=[pl.BlockSpec((n, 1, rows, depth), lambda i: (0, i, 0, 0)), full],
        out_shape=[
            jax.ShapeDtypeStruct((n, planes, rows, depth), jnp.float32),
            jax.ShapeDtypeStruct((n, n), jnp.float32),
        ],
        scratch_shapes=[pltpu.VMEM((n, 4 * n), jnp.bfloat16)],
        compiler_params=pltpu.CompilerParams(vmem_limit_bytes=24 * MIB),
        cost_estimate=pl.CostEstimate(flops=0, bytes_accessed=8 * MIB, transcendentals=0),
        name="basis",
    )(side, a, b, *tiles)


def swap(value):
    return lax.ppermute(value, "gx", [(i, i ^ 1) for i in range(lax.axis_size("gx"))])


def outward(value):
    n = lax.axis_size("gx")
    return lax.ppermute(value, "gx", [(i, i + 2 * (i % 2) * 2 - 2) for i in range(n) if 0 <= i + 4 * (i % 2) - 2 < n])


def inward(value):
    n = lax.axis_size("gx")
    return lax.ppermute(value, "gx", [(i, i + 2 - 4 * (i % 2)) for i in range(n) if 0 <= i + 2 - 4 * (i % 2) < n])


def above(value):
    n = lax.axis_size("gy")
    return lax.ppermute(value, "gy", [(i, i + 1) for i in range(n - 1)])


def below(value):
    n = lax.axis_size("gy")
    return lax.ppermute(value, "gy", [(i + 1, i) for i in range(n - 1)])


def summed(value):
    steps = []
    for axis in ("gy", "gx"):
        n = lax.axis_size(axis)
        assert n & (n - 1) == 0
        shift = 1
        while shift < n:
            steps.append((axis, shift, n))
            shift *= 2
    other = None
    for axis, shift, n in steps:
        if other is not None:
            value = value + other
        other = lax.ppermute(value, axis, [(i, i ^ shift) for i in range(n)])
    return value, other


def coefficients(side, ext, planes, rows):
    cut = EDGE - DEPTH
    k, absorb, sense, weight = ext
    depth = k.shape[2]

    def shifted(value, dx, dy):
        return value[1 + dx : value.shape[0] - 1 + dx, cut + dy : value.shape[1] - cut + dy]

    mid = shifted(k, 0, 0)
    faces = [0.5 * (mid + shifted(k, *d)) for d in ((-1, 0), (1, 0), (0, -1), (0, 1))]
    zpad = jnp.pad(mid, ((0, 0), (0, 0), (1, 1)))
    z_low = 0.5 * (mid + zpad[:, :, :-2])
    z_high = 0.5 * (mid + zpad[:, :, 2:])
    diag = shifted(absorb, 0, 0) + sum(faces) + z_low + z_high

    def inside(axis, start, total):
        index = start - DEPTH + lax.broadcasted_iota(jnp.int32, diag.shape, axis)
        return (index >= 0) & (index < total)

    gx, gy = lax.axis_index("gx"), lax.axis_index("gy")
    here = inside(0, (gx - side) * planes, planes * lax.axis_size("gx"))
    here = here & inside(1, gy * rows, rows * lax.axis_size("gy"))
    inv = jnp.where(here, OMEGA / jnp.where(here, diag, 1.0), 0.0)
    z = lax.broadcasted_iota(jnp.int32, diag.shape, 2)
    z_low = jnp.where(z == 0, 0.0, z_low)
    z_high = jnp.where(z == depth - 1, 0.0, z_high)
    sense, weight = shifted(sense, 0, 0), shifted(weight, 0, 0)
    return jnp.stack([f * inv for f in faces] + [z_low * inv, z_high * inv, sense * inv, A0 * weight * inv, A0 * sense])


def rows_of(*values):
    parts = [v.reshape(-1, v.shape[-1]) for v in values]
    return parts[0] if len(parts) == 1 else jnp.concatenate(parts, axis=0)


def fields_of(flat, *shape):
    size = 1
    for n in shape[:-1]:
        size *= n
    return flat[:size].reshape(shape)


def maps_of(flat, skip, *shape):
    return flat[skip:].reshape(shape)


def body(probes, permeability, absorption, sensitivity, observe_weight):
    count, planes, rows, depth = probes.shape
    cells = planes * lax.axis_size("gx") * rows * lax.axis_size("gy") * depth
    side = lax.axis_index("gx") % 2
    lower = side == 0
    flag = side.reshape(1).astype(jnp.int32)
    maps = (permeability, absorption, sensitivity, observe_weight)
    tall = 2 * planes + 2 * DEPTH
    assert 16 * sum(GROUPS) == count

    groups = []
    coef = turn = None
    tile = 0
    for size in GROUPS:
        mine = maps if tile == 0 else ()
        owns, sends, edges = zip(*[prep(flag, probes, tile + t, mine if t == size - 1 else ()) for t in range(size)])
        tile += size
        own, send, edge = jnp.stack(owns), rows_of(*sends), rows_of(*edges)
        if turn is not None:
            send, edge, turn = lax.optimization_barrier((send, edge, turn))
        recv = swap(send)
        e1 = outward(edge)
        turn = recv
        block, halo = (size, planes, rows, 8, depth), (size, DEPTH, rows, 8, depth)
        recv_f = fields_of(recv, *block)
        inner = [lax.dynamic_slice_in_dim(recv_f, (1 - side) * (planes - DEPTH), DEPTH, 1)]
        if mine:
            recv_m = maps_of(recv, size * planes * rows * 8, len(maps), planes, rows, depth)
            inner.append(lax.dynamic_slice_in_dim(recv_m, (1 - side) * (planes - RING), RING, 1))
        e2 = inward(rows_of(*inner))
        whole = (own, recv_f, fields_of(e1, *halo), fields_of(e2, *halo))
        low = [jnp.concatenate([p[:, :, rows - DEPTH :] for p in whole], axis=1)]
        high = [jnp.concatenate([p[:, :, :DEPTH] for p in whole], axis=1)]
        if mine:
            own_m = jnp.stack(maps)
            skip = size * DEPTH * rows * 8
            e1_m, e2_m = (maps_of(e, skip, len(maps), RING, rows, depth) for e in (e1, e2))
            wide = jnp.concatenate(
                [
                    jnp.where(lower, e2_m, e1_m),
                    jnp.where(lower, own_m, recv_m),
                    jnp.where(lower, recv_m, own_m),
                    jnp.where(lower, e1_m, e2_m),
                ],
                axis=1,
            )
            low.append(wide[:, :, rows - EDGE :])
            high.append(wide[:, :, :EDGE])
        ylo, yhi = above(rows_of(*low)), below(rows_of(*high))
        if mine:
            skip = size * tall * DEPTH * 8
            ends = [maps_of(y, skip, len(maps), tall + 2, EDGE, depth) for y in (ylo, yhi)]
            coef = coefficients(side, jnp.concatenate([ends[0], wide, ends[1]], axis=2), planes, rows)
        keep, back = solve(flag, coef, own, recv, e1, e2, ylo, yhi)
        groups.append((keep, swap(back)))
    a, b = summed(gram_of(flag, groups, cells))
    q, r = basis(flag, a, b, groups)
    return (q, r)


def solution(mesh):
    return jax.shard_map(
        body,
        mesh=mesh,
        in_specs=(
            P(None, "gx", "gy", None),
            P("gx", "gy", None),
            P("gx", "gy", None),
            P("gx", "gy", None),
            P("gx", "gy", None),
        ),
        out_specs=(P(None, "gx", "gy", None), P()),
        check_vma=False,
    )
```

```python
import functools

import jax
import jax.numpy as jnp
from jax import lax
from jax.experimental import pallas as pl
from jax.experimental.pallas import tpu as pltpu
from jax.sharding import PartitionSpec as P

OMEGA = 0.8
KEEP = 1.0 - OMEGA
A0 = 1.0 + KEEP + KEEP**2 + KEEP**3
A1 = 1.0 + 2.0 * KEEP + 3.0 * KEEP**2
A2 = 1.0 + 3.0 * KEEP
A3 = 1.0
DEPTH = 6
RING = DEPTH + 1
EDGE = 8
GROUPS = (1, 1, 1, 1)
MIB = 1 << 20


def smem():
    return pl.BlockSpec(memory_space=pltpu.SMEM)


def vmem():
    return pl.BlockSpec(memory_space=pltpu.VMEM)


def prep_kernel(h_ref, mine_ref, theirs_ref, *refs):
    maps, (own_ref, send_ref, edge_ref, wide) = refs[:-4], refs[-4:]
    planes, rows, many, depth = own_ref.shape
    side = h_ref[0]
    cells = planes * rows
    send = send_ref.at[pl.ds(0, cells * many)].reshape(own_ref.shape)
    for source, target in ((theirs_ref, send), (mine_ref, own_ref)):
        wide[...] = source[...].astype(jnp.float32).reshape(wide.shape)

        def plane(x, carry):
            for y in range(rows):
                target[x, y] = wide[pl.ds(x * rows + y, many, stride=cells), :]
            return carry

        lax.fori_loop(0, planes, plane, 0)
    edge = DEPTH * rows * many
    edge_ref[:edge] = own_ref[pl.ds(side * (planes - DEPTH), DEPTH)].reshape(edge, depth)
    for i, ref in enumerate(maps):
        at, ring = cells * many + i * cells, RING * rows
        send_ref[at : at + cells] = ref[...].reshape(cells, depth)
        part = ref[pl.ds(side * (planes - RING), RING)].reshape(ring, depth)
        edge_ref[edge + i * ring : edge + (i + 1) * ring] = part


def prep(side, probes, tile, maps):
    planes, rows, depth = probes.shape[1:]
    block = (8, planes, rows, depth)
    own = (planes, rows, 8, depth)
    send = (planes * rows * (8 + len(maps)), depth)
    edge = ((DEPTH * 8 + RING * len(maps)) * rows, depth)
    return pl.pallas_call(
        prep_kernel,
        grid_spec=pltpu.PrefetchScalarGridSpec(
            num_scalar_prefetch=1,
            grid=(1,),
            in_specs=[
                pl.BlockSpec(block, lambda i, h: (2 * tile + h[0], 0, 0, 0)),
                pl.BlockSpec(block, lambda i, h: (2 * tile + 1 - h[0], 0, 0, 0)),
            ]
            + [pl.BlockSpec(m.shape, lambda i, h: (0, 0, 0)) for m in maps],
            out_specs=[
                pl.BlockSpec(own, lambda i, h: (0, 0, 0, 0)),
                pl.BlockSpec(send, lambda i, h: (0, 0)),
                pl.BlockSpec(edge, lambda i, h: (0, 0)),
            ],
            scratch_shapes=[pltpu.VMEM((8 * planes * rows, depth), jnp.float32)],
        ),
        out_shape=[jax.ShapeDtypeStruct(s, jnp.float32) for s in (own, send, edge)],
        compiler_params=pltpu.CompilerParams(vmem_limit_bytes=16 * MIB),
        cost_estimate=pl.CostEstimate(flops=0, bytes_accessed=2 * MIB, transcendentals=0),
        name="spread_probes",
    )(side, probes, probes, *maps)


def fields_of(ref, *shape):
    size = 1
    for n in shape[:-1]:
        size *= n
    return ref.at[pl.ds(0, size)].reshape(shape)


def maps_of(ref, skip, *shape):
    size = 1
    for n in shape[:-1]:
        size *= n
    return ref.at[pl.ds(skip, size)].reshape(shape)


def map_parts(side, tiles, many, maps, recv, e1, e2):
    planes, rows, depth = maps[0].shape
    recv = maps_of(recv, tiles * planes * rows * many, len(maps), planes, rows, depth)
    e1, e2 = (maps_of(e, tiles * DEPTH * rows * many, len(maps), RING, rows, depth) for e in (e1, e2))
    top = RING + 2 * planes
    return (
        (maps, planes, RING + planes * side),
        ([recv.at[i] for i in range(len(maps))], planes, RING + planes * (1 - side)),
        ([e1.at[i] for i in range(len(maps))], RING, top * (1 - side)),
        ([e2.at[i] for i in range(len(maps))], RING, top * side),
    )


def border_kernel(h_ref, own, recv, e1, e2, *refs):
    maps, (low, high) = refs[1:-2], refs[-2:]
    tiles, planes, rows, many, depth = own.shape
    wide = 2 * planes + 2 * DEPTH
    shape = (tiles, wide, DEPTH, many, depth)
    low_f, high_f = fields_of(low, *shape), fields_of(high, *shape)
    halo = (tiles, DEPTH, rows, many, depth)
    at = 0
    for piece in (own, fields_of(recv, *own.shape), fields_of(e1, *halo), fields_of(e2, *halo)):
        for t in range(tiles):
            for i in range(piece.shape[1]):
                low_f[t, at + i] = piece[t, i, rows - DEPTH :]
                high_f[t, at + i] = piece[t, i, :DEPTH]
        at += piece.shape[1]
    if maps:
        shape = (len(maps), 2 * planes + 2 * RING, EDGE, depth)
        skip = tiles * wide * DEPTH * many
        low_m, high_m = maps_of(low, skip, *shape), maps_of(high, skip, *shape)
        for pieces, count, place in map_parts(h_ref[0], tiles, many, maps, recv, e1, e2):
            for i, piece in enumerate(pieces):
                low_m[i, pl.ds(place, count)] = piece[:, rows - EDGE :]
                high_m[i, pl.ds(place, count)] = piece[:, :EDGE]


def border(side, own, recv, e1, e2, after, maps):
    tiles, planes, rows, many, depth = own.shape
    count = tiles * (2 * planes + 2 * DEPTH) * DEPTH * many + len(maps) * (2 * planes + 2 * RING) * EDGE
    message = jax.ShapeDtypeStruct((count, depth), jnp.float32)
    return pl.pallas_call(
        border_kernel,
        in_specs=[smem()] + [vmem()] * 4 + [pl.BlockSpec(memory_space=pl.ANY)] + [vmem()] * len(maps),
        out_specs=[vmem(), vmem()],
        out_shape=[message, message],
        compiler_params=pltpu.CompilerParams(vmem_limit_bytes=12 * MIB),
        cost_estimate=pl.CostEstimate(flops=0, bytes_accessed=2 * MIB, transcendentals=0),
        name="border_rows",
    )(side, own, recv, e1, e2, after, *maps)


def coef_kernel(total_x, total_y, tiles, many, h_ref, at_ref, recv, e1, e2, ylo, yhi, *refs):
    maps, (out, ext, root) = refs[:-3], refs[-3:]
    wide_x, wide_y, depth = root.shape
    rows = maps[0].shape[1]
    skip = tiles * (wide_x - 2) * DEPTH * many
    low, high = (maps_of(y, skip, len(maps), wide_x, EDGE, depth) for y in (ylo, yhi))
    for pieces, count, place in map_parts(h_ref[0], tiles, many, maps, recv, e1, e2):
        for i, piece in enumerate(pieces):
            ext[i, pl.ds(place, count), EDGE : EDGE + rows] = piece[...]
    for i in range(len(maps)):
        ext[i, :, :EDGE] = low[i]
        ext[i, :, EDGE + rows :] = high[i]
    y = at_ref[1] + lax.broadcasted_iota(jnp.int32, (wide_y, depth), 0)
    z = lax.broadcasted_iota(jnp.int32, (wide_y, depth), 1)
    inside = (y >= 0) & (y < total_y)
    root[0] = jnp.zeros((wide_y, depth), jnp.float32)
    root[wide_x - 1] = jnp.zeros((wide_y, depth), jnp.float32)

    def roots(x, carry):
        k = ext[0, x]
        beside = ext[0, x - 1] + ext[0, x + 1] + pltpu.roll(k, 1, 0) + pltpu.roll(k, wide_y - 1, 0)
        beside = beside + jnp.where(z == 0, 0.0, pltpu.roll(k, 1, 1))
        beside = beside + jnp.where(z == depth - 1, 0.0, pltpu.roll(k, depth - 1, 1))
        diag = ext[1, x] + 0.5 * (6.0 * k + beside)
        here = inside & (at_ref[0] + x >= 0) & (at_ref[0] + x < total_x)
        root[x] = jnp.where(here, lax.rsqrt(jnp.where(here, diag, 1.0)), 0.0)
        return carry

    lax.fori_loop(1, wide_x - 1, roots, 0)

    def plane(x, carry):
        k, inv = ext[0, x], root[x]
        half = 0.5 * OMEGA * inv
        out[0, x] = half * root[x + 1] * (k + ext[0, x + 1])
        out[1, x] = half * pltpu.roll(inv, wide_y - 1, 0) * (k + pltpu.roll(k, wide_y - 1, 0))
        up = half * pltpu.roll(inv, depth - 1, 1) * (k + pltpu.roll(k, depth - 1, 1))
        out[2, x] = jnp.where(z == depth - 1, 0.0, up)
        out[3, x] = OMEGA * inv * ext[2, x]
        out[4, x] = (OMEGA * A0) * inv * inv * ext[3, x]
        out[5, x] = A0 * inv * ext[2, x]
        return carry

    lax.fori_loop(1, wide_x - 1, plane, 0)


def coefficients(side, at, totals, own, recv, e1, e2, ylo, yhi, maps):
    tiles, planes, rows, many, depth = own.shape
    wide = (2 * planes + 2 * RING, rows + 2 * EDGE, depth)
    return pl.pallas_call(
        functools.partial(coef_kernel, *totals, tiles, many),
        in_specs=[smem(), smem()] + [vmem()] * (5 + len(maps)),
        out_specs=vmem(),
        out_shape=jax.ShapeDtypeStruct((6,) + wide, jnp.float32),
        scratch_shapes=[pltpu.VMEM((len(maps),) + wide, jnp.float32), pltpu.VMEM(wide, jnp.float32)],
        compiler_params=pltpu.CompilerParams(vmem_limit_bytes=20 * MIB),
        cost_estimate=pl.CostEstimate(flops=0, bytes_accessed=4 * MIB, transcendentals=0),
        name="coefficients",
    )(side, at, recv, e1, e2, ylo, yhi, *maps)


def spread(coef, which, x, y, many):
    return coef[which, x, pl.ds(y, many, stride=0), :]


def solve_kernel(h_ref, after, coef, own, recv, e1, e2, ylo, yhi, keep, back, r_s, a_s, b_s):
    tiles, planes, rows, many, depth = own.shape
    wide_x, wide_y = r_s.shape[1], r_s.shape[2]
    side = h_ref[0]
    top = DEPTH + 2 * planes
    span = range(tiles)
    border_shape = (tiles, wide_x, DEPTH, many, depth)
    ylo, yhi = fields_of(ylo, *border_shape), fields_of(yhi, *border_shape)
    halo = (tiles, DEPTH, rows, many, depth)
    parts = (
        (own, 0, planes, DEPTH + planes * side),
        (fields_of(recv, *own.shape), planes, planes, DEPTH + planes * (1 - side)),
        (fields_of(e1, *halo), 2 * planes, DEPTH, top * (1 - side)),
        (fields_of(e2, *halo), 2 * planes + DEPTH, DEPTH, top * side),
    )

    def row(which, x, y):
        return spread(coef, which, x + RING - DEPTH, y + EDGE - DEPTH, many)

    for piece, role, count, place in parts:

        def fill(i, carry, piece=piece, role=role, place=place):
            x = place + i
            for y in range(wide_y):
                scale = row(3, x, y)
                for t in span:
                    if y < DEPTH:
                        value = ylo[t, role + i, y]
                    elif y < DEPTH + rows:
                        value = piece[t, i, y - DEPTH]
                    else:
                        value = yhi[t, role + i, y - DEPTH - rows]
                    r_s[t, x, y] = value * scale
            return carry

        lax.fori_loop(0, count, fill, 0)

    def stencil(src, r, x, low, scale, last=None):
        both = (x, x + 1)
        prev = [[src[t, p, low - 1] for t in span] for p in both]
        here = [[src[t, p, low] for t in span] for p in both]
        cy_prev = [row(1, p, low - 1) for p in both]
        for y in range(low, wide_y - low):
            after = [[src[t, p, y + 1] for t in span] for p in both]
            cx = [row(0, x + k, y) for k in (-1, 0, 1)]
            cy = [row(1, p, y) for p in both]
            values = []
            for k, p in enumerate(both):
                cz = row(2, p, y)
                end = None if last is None else row(last, p, y)
                for t in span:
                    f = here[k][t]
                    before = src[t, x - 1, y] if k == 0 else here[0][t]
                    beyond = here[1][t] if k == 0 else src[t, x + 2, y]
                    total = cx[k] * before + cx[k + 1] * beyond
                    total = total + (cy_prev[k] * prev[k][t] + cy[k] * after[k][t])
                    total = total + (pltpu.roll(cz * f, 1, 1) + cz * pltpu.roll(f, depth - 1, 1))
                    value = r[t, p, y] + scale * total
                    values.append((t, k, value if end is None else value * end))
            yield y, values
            prev, here, cy_prev = here, after, cy

    def sweep(src, dst, r, low, scale, last=None):
        def pair(i, carry):
            x = low + 2 * i
            for y, values in stencil(src, r, x, low, scale, last):
                for t, k, value in values:
                    dst[t, x + k, y] = value
            return carry

        lax.fori_loop(0, (wide_x - 2 * low) // 2, pair, 0)

    sweep(r_s, a_s, r_s, 1, A3 / A2)
    sweep(a_s, b_s, r_s, 2, A2 / A1)
    sweep(b_s, a_s, r_s, 3, A1 / A0, last=4)
    sweep(a_s, b_s, a_s, 4, A3 / A2)
    sweep(b_s, r_s, a_s, 5, A2 / A1)
    for target, place in ((back, parts[1][3]), (keep, parts[0][3])):

        def out(i, carry, target=target, place=place):
            for y, values in stencil(r_s, a_s, place + 2 * i, DEPTH, A1 / A0, last=5):
                for t, k, value in values:
                    target[t, 2 * i + k, y - DEPTH] = value
            return carry

        lax.fori_loop(0, planes // 2, out, 0)


def solve(side, after, coef, own, *messages):
    tiles, planes, rows, many, depth = own.shape
    wide = (2 * planes + 2 * DEPTH, rows + 2 * DEPTH)
    field = pltpu.VMEM((tiles,) + wide + (many, depth), jnp.float32)
    cells = tiles * wide[0] * wide[1] * many * depth
    return pl.pallas_call(
        solve_kernel,
        in_specs=[smem(), pl.BlockSpec(memory_space=pl.ANY)] + [vmem()] * 7,
        out_specs=[vmem(), vmem()],
        out_shape=[jax.ShapeDtypeStruct(own.shape, jnp.float32)] * 2,
        scratch_shapes=[field, field, field],
        compiler_params=pltpu.CompilerParams(vmem_limit_bytes=(6 + 17 * tiles) * MIB),
        cost_estimate=pl.CostEstimate(flops=60 * cells, bytes_accessed=12 * MIB, transcendentals=0),
        name="both_solves",
    )(side, after, coef, own, *messages)


def stacked(side, tiles, rows):
    columns = []
    for y in range(rows):
        parts = []
        for keep, got in zip(tiles[0::2], tiles[1::2]):
            a, b = keep[0, 0, y], got[0, 0, y]
            parts += [jnp.where(side == 0, a, b), jnp.where(side == 0, b, a)]
        columns.append(jnp.concatenate(parts, axis=0))
    return jnp.concatenate(columns, axis=1)


def split(value):
    high = value.astype(jnp.bfloat16)
    return high, (value - high.astype(jnp.float32)).astype(jnp.bfloat16)


def gram_kernel(scale, h_ref, *refs):
    tiles, out, total = refs[:-2], refs[-2], refs[-1]
    step = pl.program_id(0)

    @pl.when(step == 0)
    def _():
        total[...] = jnp.zeros_like(total)

    both = jnp.concatenate(split(stacked(h_ref[0], tiles, tiles[0].shape[2])), axis=0)
    total[...] += lax.dot_general(both, both, (((1,), (1,)), ((), ())), preferred_element_type=jnp.float32)

    @pl.when(step == pl.num_programs(0) - 1)
    def _():
        n = out.shape[0]
        g = total[:n, :n] + total[:n, n:] + total[n:, :n] + total[n:, n:]
        out[...] = g * scale


def tile_specs(groups):
    return [
        pl.BlockSpec((1, 1) + g.shape[2:], lambda i, t=t: (t, i, 0, 0, 0))
        for keep, got in groups
        for t in range(keep.shape[0])
        for g in (keep, got)
    ]


def tile_args(groups):
    return [g for keep, got in groups for t in range(keep.shape[0]) for g in (keep, got)]


def gram_of(side, groups, cells):
    tiles = tile_args(groups)
    count = 8 * len(tiles)
    return pl.pallas_call(
        functools.partial(gram_kernel, 1.0 / cells),
        grid=(tiles[0].shape[1],),
        in_specs=[smem()] + tile_specs(groups),
        out_specs=pl.BlockSpec((count, count), lambda i: (0, 0)),
        out_shape=jax.ShapeDtypeStruct((count, count), jnp.float32),
        scratch_shapes=[pltpu.VMEM((2 * count, 2 * count), jnp.float32)],
        compiler_params=pltpu.CompilerParams(vmem_limit_bytes=16 * MIB),
        cost_estimate=pl.CostEstimate(flops=0, bytes_accessed=6 * MIB, transcendentals=0),
        name="gram",
    )(side, *tiles)


def factor(gram):
    n = gram.shape[0]
    i = lax.broadcasted_iota(jnp.int32, (n, n), 0)
    j = lax.broadcasted_iota(jnp.int32, (n, n), 1)
    both = jnp.concatenate([gram, (i == j).astype(jnp.float32)], axis=1)
    rows = [both[8 * t : 8 * t + 8] for t in range(n // 8)]
    place = lax.broadcasted_iota(jnp.int32, (8, 2 * n), 0)
    for c in range(0, n, 2):
        t, s = divmod(c, 8)
        first, second = rows[t][s : s + 1], rows[t][s + 1 : s + 2]
        a, b, d = first[:, c : c + 1], first[:, c + 1 : c + 2], second[:, c + 1 : c + 2]
        inv = 1.0 / (a * d - b * b)
        w1 = (d * first - b * second) * inv
        w2 = (a * second - b * first) * inv
        fixed = jnp.where(place == s + 1, second - (b / a) * first, rows[t])
        for k in range(t, n // 8):
            new = rows[k] - (rows[k][:, c : c + 1] * w1 + rows[k][:, c + 1 : c + 2] * w2)
            rows[k] = jnp.where(place > s + 1, new, fixed) if k == t else new
    done = jnp.concatenate(rows, axis=0)
    size = jnp.sum(jnp.where(i == j, done[:, :n], 0.0), axis=1, keepdims=True)
    done = done * lax.rsqrt(size)
    return done[:, :n], done[:, n:]


def basis_kernel(h_ref, a_ref, b_ref, *refs):
    tiles, (q_ref, r_ref, left) = refs[:-3], refs[-3:]
    n = r_ref.shape[0]
    rows = tiles[0].shape[2]

    @pl.when(pl.program_id(0) == 0)
    def _():
        upper, inverse = factor(a_ref[...] + b_ref[...])
        i = lax.broadcasted_iota(jnp.int32, (n, n), 0)
        j = lax.broadcasted_iota(jnp.int32, (n, n), 1)
        r_ref[...] = jnp.where(j >= i, upper, 0.0)
        inverse = jnp.where(j <= i, inverse, 0.0)
        high, low = split(inverse)
        left[...] = jnp.concatenate([high, high, low, low], axis=1)

    high, low = split(stacked(h_ref[0], tiles, rows))
    q = jnp.dot(left[...], jnp.concatenate([high, low, high, low], axis=0), preferred_element_type=jnp.float32)
    depth = q.shape[1] // rows
    flat = q_ref.reshape(n * rows, depth)
    for y in range(rows):
        flat[pl.ds(y, n, stride=rows), :] = q[:, y * depth : (y + 1) * depth]


def basis(side, a, b, groups):
    n = a.shape[0]
    tiles = tile_args(groups)
    _, planes, rows, _, depth = tiles[0].shape
    full = pl.BlockSpec((n, n), lambda i: (0, 0))
    return pl.pallas_call(
        basis_kernel,
        grid=(planes,),
        in_specs=[smem(), full, full] + tile_specs(groups),
        out_specs=[pl.BlockSpec((n, 1, rows, depth), lambda i: (0, i, 0, 0)), full],
        out_shape=[
            jax.ShapeDtypeStruct((n, planes, rows, depth), jnp.float32),
            jax.ShapeDtypeStruct((n, n), jnp.float32),
        ],
        scratch_shapes=[pltpu.VMEM((n, 4 * n), jnp.bfloat16)],
        compiler_params=pltpu.CompilerParams(vmem_limit_bytes=24 * MIB),
        cost_estimate=pl.CostEstimate(flops=0, bytes_accessed=8 * MIB, transcendentals=0),
        name="basis",
    )(side, a, b, *tiles)


def swap(value):
    return lax.ppermute(value, "gx", [(i, i ^ 1) for i in range(lax.axis_size("gx"))])


def outward(value):
    n = lax.axis_size("gx")
    return lax.ppermute(value, "gx", [(i, i + 2 * (i % 2) * 2 - 2) for i in range(n) if 0 <= i + 4 * (i % 2) - 2 < n])


def inward(value):
    n = lax.axis_size("gx")
    return lax.ppermute(value, "gx", [(i, i + 2 - 4 * (i % 2)) for i in range(n) if 0 <= i + 2 - 4 * (i % 2) < n])


def above(value):
    n = lax.axis_size("gy")
    return lax.ppermute(value, "gy", [(i, i + 1) for i in range(n - 1)])


def below(value):
    n = lax.axis_size("gy")
    return lax.ppermute(value, "gy", [(i + 1, i) for i in range(n - 1)])


def summed(value):
    steps = []
    for axis in ("gy", "gx"):
        n = lax.axis_size(axis)
        assert n & (n - 1) == 0
        shift = 1
        while shift < n:
            steps.append((axis, shift, n))
            shift *= 2
    other = None
    for axis, shift, n in steps:
        if other is not None:
            value = value + other
        other = lax.ppermute(value, axis, [(i, i ^ shift) for i in range(n)])
    return value, other


def rows_of(*values):
    parts = [v.reshape(-1, v.shape[-1]) for v in values]
    return parts[0] if len(parts) == 1 else jnp.concatenate(parts, axis=0)


def inner_rows(side, recv, size, planes, rows, maps):
    depth = recv.shape[-1]
    cells = planes * rows
    fields = recv[: size * cells * 8].reshape(size, planes, rows * 8, depth)
    out = [lax.dynamic_slice_in_dim(fields, (1 - side) * (planes - DEPTH), DEPTH, 1)]
    if maps:
        extra = recv[size * cells * 8 :].reshape(len(maps), planes, rows, depth)
        out.append(lax.dynamic_slice_in_dim(extra, (1 - side) * (planes - RING), RING, 1))
    return rows_of(*out)


def body(probes, permeability, absorption, sensitivity, observe_weight):
    count, planes, rows, depth = probes.shape
    totals = (planes * lax.axis_size("gx"), rows * lax.axis_size("gy"))
    gx, gy = lax.axis_index("gx"), lax.axis_index("gy")
    side = gx % 2
    flag = side.reshape(1).astype(jnp.int32)
    at = jnp.stack([(gx - side) * planes - RING, gy * rows - EDGE]).astype(jnp.int32)
    maps = (permeability, absorption, sensitivity, observe_weight)
    assert 16 * sum(GROUPS) == count

    groups, backs = [], []
    coef = turn = None
    tile = 0
    for number, size in enumerate(GROUPS):
        mine = maps if tile == 0 else ()
        owns, sends, edges = zip(*[prep(flag, probes, tile + t, mine if t == size - 1 else ()) for t in range(size)])
        tile += size
        own, send, edge = jnp.stack(owns), rows_of(*sends), rows_of(*edges)
        if turn is not None:
            send, edge, turn = lax.optimization_barrier((send, edge, turn))
        recv = swap(send)
        e1 = outward(edge)
        turn = recv
        e2 = inward(inner_rows(side, recv, size, planes, rows, mine))
        after = backs[number - 2] if number >= 2 else own
        low, high = border(flag, own, recv, e1, e2, after, mine)
        ylo, yhi = above(low), below(high)
        if mine:
            coef = coefficients(flag, at, totals, own, recv, e1, e2, ylo, yhi, maps)
        after = groups[number - 2][1] if number >= 2 else own
        keep, back = solve(flag, after, coef, own, recv, e1, e2, ylo, yhi)
        backs.append(back)
        groups.append((keep, swap(back)))
    a, b = summed(gram_of(flag, groups, totals[0] * totals[1] * depth))
    q, r = basis(flag, a, b, groups)
    return (q, r)


def solution(mesh):
    return jax.shard_map(
        body,
        mesh=mesh,
        in_specs=(
            P(None, "gx", "gy", None),
            P("gx", "gy", None),
            P("gx", "gy", None),
            P("gx", "gy", None),
            P("gx", "gy", None),
        ),
        out_specs=(P(None, "gx", "gy", None), P()),
        check_vma=False,
    )
```

```python
import functools

import jax
import jax.numpy as jnp
from jax import lax
from jax.experimental import pallas as pl
from jax.experimental.pallas import tpu as pltpu
from jax.sharding import PartitionSpec as P

OMEGA = 0.8
KEEP = 1.0 - OMEGA
A0 = 1.0 + KEEP + KEEP**2 + KEEP**3
A1 = 1.0 + 2.0 * KEEP + 3.0 * KEEP**2
A2 = 1.0 + 3.0 * KEEP
A3 = 1.0
DEPTH = 6
RING = DEPTH + 1
EDGE = 8
GROUPS = (2, 2, 2, 1, 1)
AFTER = (None, 0, 1, 1, 2)
MIB = 1 << 20


def smem():
    return pl.BlockSpec(memory_space=pltpu.SMEM)


def vmem():
    return pl.BlockSpec(memory_space=pltpu.VMEM)


def prep_kernel(probes, out, wide):
    many, planes, rows, depth = probes.shape
    cells = planes * rows
    wide[...] = probes[...].astype(jnp.float32).reshape(wide.shape)

    def plane(x, carry):
        at = x * rows
        for y in range(rows):
            out[pl.ds(pl.multiple_of((at + y) * many, many), many), :] = wide[pl.ds(at + y, many, stride=cells), :]
        return carry

    lax.fori_loop(0, planes, plane, 0)


def prep(probes, tile, size, after):
    planes, rows, depth = probes.shape[1:]
    count = planes * rows * 8
    in_specs = [pl.BlockSpec((8, planes, rows, depth), lambda i: (tile + i, 0, 0, 0))]
    kernel, operands = prep_kernel, [probes]
    if after is not None:
        in_specs.insert(0, pl.BlockSpec(memory_space=pl.ANY))
        kernel, operands = (lambda _, *refs: prep_kernel(*refs)), [after, probes]
    return pl.pallas_call(
        kernel,
        grid=(size,),
        in_specs=in_specs,
        out_specs=pl.BlockSpec((count, depth), lambda i: (i, 0)),
        out_shape=jax.ShapeDtypeStruct((size * count, depth), jnp.float32),
        scratch_shapes=[pltpu.VMEM((count, depth), jnp.float32)],
        compiler_params=pltpu.CompilerParams(vmem_limit_bytes=40 * MIB),
        cost_estimate=pl.CostEstimate(flops=0, bytes_accessed=size * MIB, transcendentals=0),
        name="spread_probes",
    )(*operands)


def pieces_of(side, tiles, planes, rows, many, own, recv, outer):
    depth = own.shape[-1]
    own, recv = (ref.reshape(tiles, planes, rows, many, depth) for ref in (own, recv))
    outer = outer.reshape(tiles, DEPTH, rows, many, depth)
    top = DEPTH + planes
    return (
        (own, 0, planes, 0, DEPTH),
        (recv, side * (planes - DEPTH), DEPTH, planes, top * (1 - side)),
        (outer, 0, DEPTH, planes + DEPTH, top * side),
    )


def border_kernel(sizes, h_ref, own, recv, outer, after, low, high):
    tiles, planes, rows, many = sizes
    shape = (tiles, planes + 2 * DEPTH, DEPTH, many, own.shape[-1])
    low, high = low.reshape(shape), high.reshape(shape)
    for piece, first, count, role, _ in pieces_of(h_ref[0], *sizes, own, recv, outer):
        for t in range(tiles):
            for i in range(count):
                low[t, role + i] = piece[t, first + i, rows - DEPTH :]
                high[t, role + i] = piece[t, first + i, :DEPTH]


def border(side, sizes, own, recv, outer, after):
    tiles, planes, rows, many = sizes
    message = jax.ShapeDtypeStruct((tiles * (planes + 2 * DEPTH) * DEPTH * many, own.shape[-1]), jnp.float32)
    return pl.pallas_call(
        functools.partial(border_kernel, sizes),
        in_specs=[smem()] + [vmem()] * 3 + [pl.BlockSpec(memory_space=pl.ANY)],
        out_specs=[vmem(), vmem()],
        out_shape=[message, message],
        compiler_params=pltpu.CompilerParams(vmem_limit_bytes=12 * MIB),
        cost_estimate=pl.CostEstimate(flops=0, bytes_accessed=2 * MIB, transcendentals=0),
        name="border_rows",
    )(side, own, recv, outer, after)


def coef_kernel(total_x, total_y, at_ref, ext, out, root):
    wide_x, wide_y, depth = root.shape
    y = at_ref[1] + lax.broadcasted_iota(jnp.int32, (wide_y, depth), 0)
    z = lax.broadcasted_iota(jnp.int32, (wide_y, depth), 1)
    inside = (y >= 0) & (y < total_y)
    root[0] = jnp.zeros((wide_y, depth), jnp.float32)
    root[wide_x - 1] = jnp.zeros((wide_y, depth), jnp.float32)

    def roots(i, carry):
        for x in (2 * i + 1, 2 * i + 2):
            k = ext[0, x]
            beside = ext[0, x - 1] + ext[0, x + 1] + pltpu.roll(k, 1, 0) + pltpu.roll(k, wide_y - 1, 0)
            beside = beside + jnp.where(z == 0, 0.0, pltpu.roll(k, 1, 1))
            beside = beside + jnp.where(z == depth - 1, 0.0, pltpu.roll(k, depth - 1, 1))
            diag = ext[1, x] + 0.5 * (6.0 * k + beside)
            here = inside & (at_ref[0] + x >= 0) & (at_ref[0] + x < total_x)
            root[x] = jnp.where(here, lax.rsqrt(jnp.where(here, diag, 1.0)), 0.0)
        return carry

    lax.fori_loop(0, (wide_x - 2) // 2, roots, 0)

    def plane(i, carry):
        for x in (2 * i + 1, 2 * i + 2):
            k, inv = ext[0, x], root[x]
            half = 0.5 * OMEGA * inv
            out[0, x] = half * root[x + 1] * (k + ext[0, x + 1])
            out[1, x] = half * pltpu.roll(inv, wide_y - 1, 0) * (k + pltpu.roll(k, wide_y - 1, 0))
            up = half * pltpu.roll(inv, depth - 1, 1) * (k + pltpu.roll(k, depth - 1, 1))
            out[2, x] = jnp.where(z == depth - 1, 0.0, up)
            out[3, x] = OMEGA * inv * ext[2, x]
            out[4, x] = (OMEGA * A0) * inv * inv * ext[3, x]
            out[5, x] = A0 * inv * ext[2, x]
        return carry

    lax.fori_loop(0, (wide_x - 2) // 2, plane, 0)


def coefficients(side, at, totals, maps):
    planes, rows, depth = maps[0].shape
    lower = side == 0
    own = jnp.stack(maps)
    recv = swap(own)
    outer = relay(lax.dynamic_slice_in_dim(recv, (1 - side) * (planes - RING), RING, 1))
    inner = lax.dynamic_slice_in_dim(recv, side * (planes - RING), RING, 1)
    wide = jnp.concatenate([jnp.where(lower, outer, inner), own, jnp.where(lower, inner, outer)], axis=1)
    low, high = above(wide[:, :, rows - EDGE :]), below(wide[:, :, :EDGE])
    ext = jnp.concatenate([low, wide, high], axis=2)
    shape = ext.shape[1:]
    return pl.pallas_call(
        functools.partial(coef_kernel, *totals),
        in_specs=[smem(), vmem()],
        out_specs=vmem(),
        out_shape=jax.ShapeDtypeStruct((6,) + shape, jnp.float32),
        scratch_shapes=[pltpu.VMEM(shape, jnp.float32)],
        compiler_params=pltpu.CompilerParams(vmem_limit_bytes=12 * MIB),
        cost_estimate=pl.CostEstimate(flops=0, bytes_accessed=4 * MIB, transcendentals=0),
        name="coefficients",
    )(at, ext)


def spread(coef, which, x, y, many):
    return coef[which, x, pl.ds(y, many, stride=0), :]


def solve_kernel(sizes, h_ref, coef, own, recv, outer, ylo, yhi, out_ref, r_s, a_s, b_s):
    tiles, planes, rows, many = sizes
    wide_x, wide_y, _, depth = r_s.shape[1:]
    span = range(tiles)
    shape = (tiles, wide_x, DEPTH, many, depth)
    ylo, yhi = ylo.reshape(shape), yhi.reshape(shape)

    def row(which, x, y):
        return spread(coef, which, x + RING - DEPTH, y + EDGE - DEPTH, many)

    for piece, first, count, role, place in pieces_of(h_ref[0], *sizes, own, recv, outer):

        def fill(i, carry, piece=piece, first=first, role=role, place=place):
            x = place + i
            for y in range(wide_y):
                scale = row(3, x, y)
                for t in span:
                    if y < DEPTH:
                        value = ylo[t, role + i, y]
                    elif y < DEPTH + rows:
                        value = piece[t, first + i, y - DEPTH]
                    else:
                        value = yhi[t, role + i, y - DEPTH - rows]
                    r_s[t, x, y] = value * scale
            return carry

        lax.fori_loop(0, count, fill, 0)

    def stencil(src, r, x, low, scale, last=None):
        both = (x, x + 1)
        prev = [[src[t, p, low - 1] for t in span] for p in both]
        here = [[src[t, p, low] for t in span] for p in both]
        cy_prev = [row(1, p, low - 1) for p in both]
        for y in range(low, wide_y - low):
            after = [[src[t, p, y + 1] for t in span] for p in both]
            cx = [row(0, x + k, y) for k in (-1, 0, 1)]
            cy = [row(1, p, y) for p in both]
            values = []
            for k, p in enumerate(both):
                cz = row(2, p, y)
                end = None if last is None else row(last, p, y)
                for t in span:
                    f = here[k][t]
                    before = src[t, x - 1, y] if k == 0 else here[0][t]
                    beyond = here[1][t] if k == 0 else src[t, x + 2, y]
                    total = cx[k] * before + cx[k + 1] * beyond
                    total = total + (cy_prev[k] * prev[k][t] + cy[k] * after[k][t])
                    total = total + (pltpu.roll(cz * f, 1, 1) + cz * pltpu.roll(f, depth - 1, 1))
                    value = r[t, p, y] + scale * total
                    values.append((t, k, value if end is None else value * end))
            yield y, values
            prev, here, cy_prev = here, after, cy

    def sweep(src, dst, r, low, scale, last=None):
        def pair(i, carry):
            x = low + 2 * i
            for y, values in stencil(src, r, x, low, scale, last):
                for t, k, value in values:
                    dst[t, x + k, y] = value
            return carry

        lax.fori_loop(0, (wide_x - 2 * low) // 2, pair, 0)

    sweep(r_s, a_s, r_s, 1, A3 / A2)
    sweep(a_s, b_s, r_s, 2, A2 / A1)
    sweep(b_s, a_s, r_s, 3, A1 / A0, last=4)
    sweep(a_s, b_s, a_s, 4, A3 / A2)
    sweep(b_s, r_s, a_s, 5, A2 / A1)

    def out(i, carry):
        for y, values in stencil(r_s, a_s, DEPTH + 2 * i, DEPTH, A1 / A0, last=5):
            for t, k, value in values:
                out_ref[t, 2 * i + k, y - DEPTH] = value
        return carry

    lax.fori_loop(0, planes // 2, out, 0)


def solve(side, sizes, coef, *messages):
    tiles, planes, rows, many = sizes
    depth = coef.shape[-1]
    wide = (planes + 2 * DEPTH, rows + 2 * DEPTH)
    field = pltpu.VMEM((tiles,) + wide + (many, depth), jnp.float32)
    cells = tiles * wide[0] * wide[1] * many * depth
    return pl.pallas_call(
        functools.partial(solve_kernel, sizes),
        in_specs=[smem()] + [vmem()] * 6,
        out_specs=vmem(),
        out_shape=jax.ShapeDtypeStruct((tiles, planes, rows, many, depth), jnp.float32),
        scratch_shapes=[field, field, field],
        compiler_params=pltpu.CompilerParams(vmem_limit_bytes=(6 + 12 * tiles) * MIB),
        cost_estimate=pl.CostEstimate(flops=60 * cells, bytes_accessed=12 * MIB, transcendentals=0),
        name="both_solves",
    )(side, coef, *messages)


def stacked(tiles, rows):
    columns = [jnp.concatenate([t[0, 0, y] for t in tiles], axis=0) for y in range(rows)]
    return jnp.concatenate(columns, axis=1)


def split(value):
    high = value.astype(jnp.bfloat16)
    return high, (value - high.astype(jnp.float32)).astype(jnp.bfloat16)


def gram_kernel(scale, *refs):
    tiles, out, total = refs[:-2], refs[-2], refs[-1]
    step = pl.program_id(0)

    @pl.when(step == 0)
    def _():
        total[...] = jnp.zeros_like(total)

    both = jnp.concatenate(split(stacked(tiles, tiles[0].shape[2])), axis=0)
    total[...] += lax.dot_general(both, both, (((1,), (1,)), ((), ())), preferred_element_type=jnp.float32)

    @pl.when(step == pl.num_programs(0) - 1)
    def _():
        n = out.shape[0]
        g = total[:n, :n] + total[:n, n:] + total[n:, :n] + total[n:, n:]
        out[...] = g * scale


def tile_specs(groups):
    return [
        pl.BlockSpec((1, 1) + g.shape[2:], lambda i, t=t: (t, i, 0, 0, 0)) for g in groups for t in range(g.shape[0])
    ]


def tile_args(groups):
    return [g for g in groups for t in range(g.shape[0])]


def gram_of(groups, cells):
    tiles = tile_args(groups)
    count = 8 * len(tiles)
    return pl.pallas_call(
        functools.partial(gram_kernel, 1.0 / cells),
        grid=(tiles[0].shape[1],),
        in_specs=tile_specs(groups),
        out_specs=pl.BlockSpec((count, count), lambda i: (0, 0)),
        out_shape=jax.ShapeDtypeStruct((count, count), jnp.float32),
        scratch_shapes=[pltpu.VMEM((2 * count, 2 * count), jnp.float32)],
        compiler_params=pltpu.CompilerParams(vmem_limit_bytes=16 * MIB),
        cost_estimate=pl.CostEstimate(flops=0, bytes_accessed=6 * MIB, transcendentals=0),
        name="gram",
    )(*tiles)


def factor(gram):
    n = gram.shape[0]
    i = lax.broadcasted_iota(jnp.int32, (n, n), 0)
    j = lax.broadcasted_iota(jnp.int32, (n, n), 1)
    both = jnp.concatenate([gram, (i == j).astype(jnp.float32)], axis=1)
    rows = [both[8 * t : 8 * t + 8] for t in range(n // 8)]
    place = lax.broadcasted_iota(jnp.int32, (8, 2 * n), 0)
    for c in range(0, n, 2):
        t, s = divmod(c, 8)
        first, second = rows[t][s : s + 1], rows[t][s + 1 : s + 2]
        a, b, d = first[:, c : c + 1], first[:, c + 1 : c + 2], second[:, c + 1 : c + 2]
        inv = 1.0 / (a * d - b * b)
        w1 = (d * first - b * second) * inv
        w2 = (a * second - b * first) * inv
        fixed = jnp.where(place == s + 1, second - (b / a) * first, rows[t])
        for k in range(t, n // 8):
            new = rows[k] - (rows[k][:, c : c + 1] * w1 + rows[k][:, c + 1 : c + 2] * w2)
            rows[k] = jnp.where(place > s + 1, new, fixed) if k == t else new
    done = jnp.concatenate(rows, axis=0)
    size = jnp.sum(jnp.where(i == j, done[:, :n], 0.0), axis=1, keepdims=True)
    done = done * lax.rsqrt(size)
    return done[:, :n], done[:, n:]


def basis_kernel(a_ref, b_ref, *refs):
    tiles, (q_ref, r_ref, left) = refs[:-3], refs[-3:]
    n = r_ref.shape[0]
    rows = tiles[0].shape[2]

    @pl.when(pl.program_id(0) == 0)
    def _():
        upper, inverse = factor(a_ref[...] + b_ref[...])
        i = lax.broadcasted_iota(jnp.int32, (n, n), 0)
        j = lax.broadcasted_iota(jnp.int32, (n, n), 1)
        r_ref[...] = jnp.where(j >= i, upper, 0.0)
        inverse = jnp.where(j <= i, inverse, 0.0)
        high, low = split(inverse)
        left[...] = jnp.concatenate([high, high, low, low], axis=1)

    high, low = split(stacked(tiles, rows))
    q = jnp.dot(left[...], jnp.concatenate([high, low, high, low], axis=0), preferred_element_type=jnp.float32)
    depth = q.shape[1] // rows
    flat = q_ref.reshape(n * rows, depth)
    for y in range(rows):
        flat[pl.ds(y, n, stride=rows), :] = q[:, y * depth : (y + 1) * depth]


def basis(a, b, groups):
    n = a.shape[0]
    tiles = tile_args(groups)
    _, planes, rows, _, depth = tiles[0].shape
    full = pl.BlockSpec((n, n), lambda i: (0, 0))
    return pl.pallas_call(
        basis_kernel,
        grid=(planes,),
        in_specs=[full, full] + tile_specs(groups),
        out_specs=[pl.BlockSpec((n, 1, rows, depth), lambda i: (0, i, 0, 0)), full],
        out_shape=[
            jax.ShapeDtypeStruct((n, planes, rows, depth), jnp.float32),
            jax.ShapeDtypeStruct((n, n), jnp.float32),
        ],
        scratch_shapes=[pltpu.VMEM((n, 4 * n), jnp.bfloat16)],
        compiler_params=pltpu.CompilerParams(vmem_limit_bytes=24 * MIB),
        cost_estimate=pl.CostEstimate(flops=0, bytes_accessed=8 * MIB, transcendentals=0),
        name="basis",
    )(a, b, *tiles)


def swap(value):
    return lax.ppermute(value, "gx", [(i, i ^ 1) for i in range(lax.axis_size("gx"))])


def relay(value):
    n = lax.axis_size("gx")
    return lax.ppermute(value, "gx", [(i, i + 2 - 4 * (i % 2)) for i in range(n) if 0 <= i + 2 - 4 * (i % 2) < n])


def above(value):
    n = lax.axis_size("gy")
    return lax.ppermute(value, "gy", [(i, i + 1) for i in range(n - 1)])


def below(value):
    n = lax.axis_size("gy")
    return lax.ppermute(value, "gy", [(i + 1, i) for i in range(n - 1)])


def summed(value):
    steps = []
    for axis in ("gy", "gx"):
        n = lax.axis_size(axis)
        assert n & (n - 1) == 0
        shift = 1
        while shift < n:
            steps.append((axis, shift, n))
            shift *= 2
    other = None
    for axis, shift, n in steps:
        if other is not None:
            value = value + other
        other = lax.ppermute(value, axis, [(i, i ^ shift) for i in range(n)])
    return value, other


def relayed(side, recv, size, planes):
    fields = recv.reshape(size, planes, -1, recv.shape[-1])
    part = lax.dynamic_slice_in_dim(fields, (1 - side) * (planes - DEPTH), DEPTH, 1)
    return relay(part.reshape(-1, recv.shape[-1]))


def body(probes, permeability, absorption, sensitivity, observe_weight):
    count, planes, rows, depth = probes.shape
    totals = (planes * lax.axis_size("gx"), rows * lax.axis_size("gy"))
    gx, gy = lax.axis_index("gx"), lax.axis_index("gy")
    side = gx % 2
    flag = side.reshape(1).astype(jnp.int32)
    at = jnp.stack([gx * planes - RING, gy * rows - EDGE]).astype(jnp.int32)
    assert 8 * sum(GROUPS) == count

    groups = []
    coef = recv = None
    tile = 0
    for number, size in enumerate(GROUPS):
        sizes = (size, planes, rows, 8)
        own = prep(probes, tile, size, recv)
        tile += size
        recv = swap(own)
        if coef is None:
            coef = coefficients(side, at, totals, (permeability, absorption, sensitivity, observe_weight))
        outer = relayed(side, recv, size, planes)
        after = AFTER[number]
        low, high = border(flag, sizes, own, recv, outer, own if after is None else groups[after])
        groups.append(solve(flag, sizes, coef, own, recv, outer, above(low), below(high)))
    a, b = summed(gram_of(groups, totals[0] * totals[1] * depth))
    q, r = basis(a, b, groups)
    return (q, r)


def solution(mesh):
    return jax.shard_map(
        body,
        mesh=mesh,
        in_specs=(
            P(None, "gx", "gy", None),
            P("gx", "gy", None),
            P("gx", "gy", None),
            P("gx", "gy", None),
            P("gx", "gy", None),
        ),
        out_specs=(P(None, "gx", "gy", None), P()),
        check_vma=False,
    )
```

```python
import functools

import jax
import jax.numpy as jnp
from jax import lax
from jax.experimental import pallas as pl
from jax.experimental.pallas import tpu as pltpu
from jax.sharding import PartitionSpec as P

OMEGA = 0.8
KEEP = 1.0 - OMEGA
A0 = 1.0 + KEEP + KEEP**2 + KEEP**3
A1 = 1.0 + 2.0 * KEEP + 3.0 * KEEP**2
A2 = 1.0 + 3.0 * KEEP
A3 = 1.0
DEPTH = 6
RING = DEPTH + 1
EDGE = 8
GROUPS = (1, 2, 2, 2, 1)
AFTER = (None, 0, 1, 1, 2)
BLOCK = 4
MIB = 1 << 20


def smem():
    return pl.BlockSpec(memory_space=pltpu.SMEM)


def vmem():
    return pl.BlockSpec(memory_space=pltpu.VMEM)


def prep_kernel(probes, out, wide):
    many, planes, rows, depth = probes.shape
    cells = planes * rows
    wide[...] = probes[...].astype(jnp.float32).reshape(wide.shape)

    def plane(x, carry):
        at = x * rows
        for y in range(rows):
            out[pl.ds(pl.multiple_of((at + y) * many, many), many), :] = wide[pl.ds(at + y, many, stride=cells), :]
        return carry

    lax.fori_loop(0, planes, plane, 0)


def prep(probes, tile, size):
    planes, rows, depth = probes.shape[1:]
    count = planes * rows * 8
    return pl.pallas_call(
        prep_kernel,
        grid=(size,),
        in_specs=[pl.BlockSpec((8, planes, rows, depth), lambda i: (tile + i, 0, 0, 0))],
        out_specs=pl.BlockSpec((count, depth), lambda i: (i, 0)),
        out_shape=jax.ShapeDtypeStruct((size * count, depth), jnp.float32),
        scratch_shapes=[pltpu.VMEM((count, depth), jnp.float32)],
        compiler_params=pltpu.CompilerParams(vmem_limit_bytes=40 * MIB),
        cost_estimate=pl.CostEstimate(flops=0, bytes_accessed=size * MIB, transcendentals=0),
        name="spread_probes",
    )(probes)


def pieces_of(side, tiles, planes, rows, many, own, recv, outer):
    depth = own.shape[-1]
    own, recv = (ref.reshape(tiles, planes, rows, many, depth) for ref in (own, recv))
    outer = outer.reshape(tiles, DEPTH, rows, many, depth)
    top = DEPTH + planes
    return (
        (own, 0, planes, 0, DEPTH),
        (recv, side * (planes - DEPTH), DEPTH, planes, top * (1 - side)),
        (outer, 0, DEPTH, planes + DEPTH, top * side),
    )


def border_kernel(sizes, h_ref, own, recv, outer, after, low, high):
    tiles, planes, rows, many = sizes
    shape = (tiles, planes + 2 * DEPTH, DEPTH, many, own.shape[-1])
    low, high = low.reshape(shape), high.reshape(shape)
    for piece, first, count, role, _ in pieces_of(h_ref[0], *sizes, own, recv, outer):
        for t in range(tiles):
            for i in range(count):
                low[t, role + i] = piece[t, first + i, rows - DEPTH :]
                high[t, role + i] = piece[t, first + i, :DEPTH]


def border(side, sizes, own, recv, outer, after):
    tiles, planes, rows, many = sizes
    message = jax.ShapeDtypeStruct((tiles * (planes + 2 * DEPTH) * DEPTH * many, own.shape[-1]), jnp.float32)
    return pl.pallas_call(
        functools.partial(border_kernel, sizes),
        in_specs=[smem()] + [vmem()] * 3 + [pl.BlockSpec(memory_space=pl.ANY)],
        out_specs=[vmem(), vmem()],
        out_shape=[message, message],
        compiler_params=pltpu.CompilerParams(vmem_limit_bytes=12 * MIB),
        cost_estimate=pl.CostEstimate(flops=0, bytes_accessed=2 * MIB, transcendentals=0),
        name="border_rows",
    )(side, own, recv, outer, after)


def coef_kernel(total_x, total_y, at_ref, ext, out, root):
    wide_x, wide_y, depth = root.shape
    y = at_ref[1] + lax.broadcasted_iota(jnp.int32, (wide_y, depth), 0)
    z = lax.broadcasted_iota(jnp.int32, (wide_y, depth), 1)
    inside = (y >= 0) & (y < total_y)
    root[0] = jnp.zeros((wide_y, depth), jnp.float32)
    root[wide_x - 1] = jnp.zeros((wide_y, depth), jnp.float32)

    def roots(i, carry):
        for x in (2 * i + 1, 2 * i + 2):
            k = ext[0, x]
            beside = ext[0, x - 1] + ext[0, x + 1] + pltpu.roll(k, 1, 0) + pltpu.roll(k, wide_y - 1, 0)
            beside = beside + jnp.where(z == 0, 0.0, pltpu.roll(k, 1, 1))
            beside = beside + jnp.where(z == depth - 1, 0.0, pltpu.roll(k, depth - 1, 1))
            diag = ext[1, x] + 0.5 * (6.0 * k + beside)
            here = inside & (at_ref[0] + x >= 0) & (at_ref[0] + x < total_x)
            root[x] = jnp.where(here, lax.rsqrt(jnp.where(here, diag, 1.0)), 0.0)
        return carry

    lax.fori_loop(0, (wide_x - 2) // 2, roots, 0)

    def plane(i, carry):
        for x in (2 * i + 1, 2 * i + 2):
            k, inv = ext[0, x], root[x]
            half = 0.5 * OMEGA * inv
            out[0, x] = half * root[x + 1] * (k + ext[0, x + 1])
            out[1, x] = half * pltpu.roll(inv, wide_y - 1, 0) * (k + pltpu.roll(k, wide_y - 1, 0))
            up = half * pltpu.roll(inv, depth - 1, 1) * (k + pltpu.roll(k, depth - 1, 1))
            out[2, x] = jnp.where(z == depth - 1, 0.0, up)
            out[3, x] = OMEGA * inv * ext[2, x]
            out[4, x] = (OMEGA * A0) * inv * inv * ext[3, x]
            out[5, x] = A0 * inv * ext[2, x]
        return carry

    lax.fori_loop(0, (wide_x - 2) // 2, plane, 0)


def widened(side, maps, after):
    planes, rows, depth = maps[0].shape
    lower = side == 0
    own = once(jnp.stack(maps), after)
    recv = swap(own)
    outer = relay(lax.dynamic_slice_in_dim(recv, (1 - side) * (planes - RING), RING, 1))
    inner = lax.dynamic_slice_in_dim(recv, side * (planes - RING), RING, 1)
    wide = jnp.concatenate([jnp.where(lower, outer, inner), own, jnp.where(lower, inner, outer)], axis=1)
    low, high = above(wide[:, :, rows - EDGE :]), below(wide[:, :, :EDGE])
    return jnp.concatenate([low, wide, high], axis=2), recv, wide


def coefficients(at, totals, ext):
    shape = ext.shape[1:]
    return pl.pallas_call(
        functools.partial(coef_kernel, *totals),
        in_specs=[smem(), vmem()],
        out_specs=vmem(),
        out_shape=jax.ShapeDtypeStruct((6,) + shape, jnp.float32),
        scratch_shapes=[pltpu.VMEM(shape, jnp.float32)],
        compiler_params=pltpu.CompilerParams(vmem_limit_bytes=12 * MIB),
        cost_estimate=pl.CostEstimate(flops=0, bytes_accessed=4 * MIB, transcendentals=0),
        name="coefficients",
    )(at, ext)


def spread(coef, which, x, y, many):
    return coef[which, x, pl.ds(y, many, stride=0), :]


def solve_kernel(sizes, h_ref, coef, own, recv, outer, ylo, yhi, out_ref, r_s, a_s, b_s):
    tiles, planes, rows, many = sizes
    wide_x, wide_y, _, depth = r_s.shape[1:]
    span = range(tiles)
    shape = (tiles, wide_x, DEPTH, many, depth)
    ylo, yhi = ylo.reshape(shape), yhi.reshape(shape)

    def row(which, x, y):
        return spread(coef, which, x + RING - DEPTH, y + EDGE - DEPTH, many)

    for piece, first, count, role, place in pieces_of(h_ref[0], *sizes, own, recv, outer):

        def fill(i, carry, piece=piece, first=first, role=role, place=place):
            x = place + i
            for y in range(wide_y):
                scale = row(3, x, y)
                for t in span:
                    if y < DEPTH:
                        value = ylo[t, role + i, y]
                    elif y < DEPTH + rows:
                        value = piece[t, first + i, y - DEPTH]
                    else:
                        value = yhi[t, role + i, y - DEPTH - rows]
                    r_s[t, x, y] = value * scale
            return carry

        lax.fori_loop(0, count, fill, 0)

    def stencil(src, r, x, block, low, scale, last=None):
        inner = range(block)
        prev = [[src[t, x + k, low - 1] for t in span] for k in inner]
        here = [[src[t, x + k, low] for t in span] for k in inner]
        cy_prev = [row(1, x + k, low - 1) for k in inner]
        for y in range(low, wide_y - low):
            after = [[src[t, x + k, y + 1] for t in span] for k in inner]
            cx = [row(0, x + k, y) for k in range(-1, block)]
            cy = [row(1, x + k, y) for k in inner]
            values = []
            for k in inner:
                cz = row(2, x + k, y)
                end = None if last is None else row(last, x + k, y)
                for t in span:
                    f = here[k][t]
                    before = here[k - 1][t] if k else src[t, x - 1, y]
                    beyond = here[k + 1][t] if k + 1 < block else src[t, x + block, y]
                    total = cx[k] * before + cx[k + 1] * beyond
                    total = total + (cy_prev[k] * prev[k][t] + cy[k] * after[k][t])
                    total = total + (pltpu.roll(cz * f, 1, 1) + cz * pltpu.roll(f, depth - 1, 1))
                    value = r[t, x + k, y] + scale * total
                    values.append((t, k, value if end is None else value * end))
            yield y, values
            prev, here, cy_prev = here, after, cy

    def sweep(src, dst, r, low, scale, last=None):
        def planes_at(x, block):
            for y, values in stencil(src, r, x, block, low, scale, last):
                for t, k, value in values:
                    dst[t, x + k, y] = value

        def step(i, carry):
            planes_at(low + BLOCK * i, BLOCK)
            return carry

        full, rest = divmod(wide_x - 2 * low, BLOCK)
        lax.fori_loop(0, full, step, 0)
        if rest:
            planes_at(low + BLOCK * full, rest)

    sweep(r_s, a_s, r_s, 1, A3 / A2)
    sweep(a_s, b_s, r_s, 2, A2 / A1)
    sweep(b_s, a_s, r_s, 3, A1 / A0, last=4)
    sweep(a_s, b_s, a_s, 4, A3 / A2)
    sweep(b_s, r_s, a_s, 5, A2 / A1)

    def out(i, carry):
        for y, values in stencil(r_s, a_s, DEPTH + BLOCK * i, BLOCK, DEPTH, A1 / A0, last=5):
            for t, k, value in values:
                out_ref[t, BLOCK * i + k, y - DEPTH] = value
        return carry

    lax.fori_loop(0, planes // BLOCK, out, 0)


def solve(side, sizes, coef, *messages):
    tiles, planes, rows, many = sizes
    depth = coef.shape[-1]
    wide = (planes + 2 * DEPTH, rows + 2 * DEPTH)
    field = pltpu.VMEM((tiles,) + wide + (many, depth), jnp.float32)
    cells = tiles * wide[0] * wide[1] * many * depth
    return pl.pallas_call(
        functools.partial(solve_kernel, sizes),
        in_specs=[smem()] + [vmem()] * 6,
        out_specs=vmem(),
        out_shape=jax.ShapeDtypeStruct((tiles, planes, rows, many, depth), jnp.float32),
        scratch_shapes=[field, field, field],
        compiler_params=pltpu.CompilerParams(vmem_limit_bytes=(6 + 12 * tiles) * MIB),
        cost_estimate=pl.CostEstimate(flops=60 * cells, bytes_accessed=12 * MIB, transcendentals=0),
        name="both_solves",
    )(side, coef, *messages)


def stacked(tiles, rows):
    columns = [jnp.concatenate([t[0, 0, y] for t in tiles], axis=0) for y in range(rows)]
    return jnp.concatenate(columns, axis=1)


def split(value):
    high = value.astype(jnp.bfloat16)
    return high, (value - high.astype(jnp.float32)).astype(jnp.bfloat16)


def gram_kernel(scale, *refs):
    tiles, out, total = refs[:-2], refs[-2], refs[-1]
    step = pl.program_id(0)

    @pl.when(step == 0)
    def _():
        total[...] = jnp.zeros_like(total)

    both = jnp.concatenate(split(stacked(tiles, tiles[0].shape[2])), axis=0)
    total[...] += lax.dot_general(both, both, (((1,), (1,)), ((), ())), preferred_element_type=jnp.float32)

    @pl.when(step == pl.num_programs(0) - 1)
    def _():
        n = out.shape[0]
        g = total[:n, :n] + total[:n, n:] + total[n:, :n] + total[n:, n:]
        out[...] = g * scale


def tile_specs(groups):
    return [
        pl.BlockSpec((1, 1) + g.shape[2:], lambda i, t=t: (t, i, 0, 0, 0)) for g in groups for t in range(g.shape[0])
    ]


def tile_args(groups):
    return [g for g in groups for t in range(g.shape[0])]


def gram_of(groups, cells):
    tiles = tile_args(groups)
    count = 8 * len(tiles)
    return pl.pallas_call(
        functools.partial(gram_kernel, 1.0 / cells),
        grid=(tiles[0].shape[1],),
        in_specs=tile_specs(groups),
        out_specs=pl.BlockSpec((count, count), lambda i: (0, 0)),
        out_shape=jax.ShapeDtypeStruct((count, count), jnp.float32),
        scratch_shapes=[pltpu.VMEM((2 * count, 2 * count), jnp.float32)],
        compiler_params=pltpu.CompilerParams(vmem_limit_bytes=16 * MIB),
        cost_estimate=pl.CostEstimate(flops=0, bytes_accessed=6 * MIB, transcendentals=0),
        name="gram",
    )(*tiles)


def factor(gram):
    n = gram.shape[0]
    i = lax.broadcasted_iota(jnp.int32, (n, n), 0)
    j = lax.broadcasted_iota(jnp.int32, (n, n), 1)
    both = jnp.concatenate([gram, (i == j).astype(jnp.float32)], axis=1)
    rows = [both[8 * t : 8 * t + 8] for t in range(n // 8)]
    place = lax.broadcasted_iota(jnp.int32, (8, 2 * n), 0)
    for c in range(0, n, 2):
        t, s = divmod(c, 8)
        first, second = rows[t][s : s + 1], rows[t][s + 1 : s + 2]
        a, b, d = first[:, c : c + 1], first[:, c + 1 : c + 2], second[:, c + 1 : c + 2]
        inv = 1.0 / (a * d - b * b)
        w1 = (d * first - b * second) * inv
        w2 = (a * second - b * first) * inv
        fixed = jnp.where(place == s + 1, second - (b / a) * first, rows[t])
        for k in range(t, n // 8):
            new = rows[k] - (rows[k][:, c : c + 1] * w1 + rows[k][:, c + 1 : c + 2] * w2)
            rows[k] = jnp.where(place > s + 1, new, fixed) if k == t else new
    done = jnp.concatenate(rows, axis=0)
    size = jnp.sum(jnp.where(i == j, done[:, :n], 0.0), axis=1, keepdims=True)
    done = done * lax.rsqrt(size)
    return done[:, :n], done[:, n:]


def basis_kernel(a_ref, b_ref, *refs):
    tiles, (q_ref, r_ref, left) = refs[:-3], refs[-3:]
    n = r_ref.shape[0]
    rows = tiles[0].shape[2]

    @pl.when(pl.program_id(0) == 0)
    def _():
        upper, inverse = factor(a_ref[...] + b_ref[...])
        i = lax.broadcasted_iota(jnp.int32, (n, n), 0)
        j = lax.broadcasted_iota(jnp.int32, (n, n), 1)
        r_ref[...] = jnp.where(j >= i, upper, 0.0)
        inverse = jnp.where(j <= i, inverse, 0.0)
        high, low = split(inverse)
        left[...] = jnp.concatenate([high, high, low, low], axis=1)

    high, low = split(stacked(tiles, rows))
    q = jnp.dot(left[...], jnp.concatenate([high, low, high, low], axis=0), preferred_element_type=jnp.float32)
    depth = q.shape[1] // rows
    flat = q_ref.reshape(n * rows, depth)
    for y in range(rows):
        flat[pl.ds(y, n, stride=rows), :] = q[:, y * depth : (y + 1) * depth]


def basis(a, b, groups):
    n = a.shape[0]
    tiles = tile_args(groups)
    _, planes, rows, _, depth = tiles[0].shape
    full = pl.BlockSpec((n, n), lambda i: (0, 0))
    return pl.pallas_call(
        basis_kernel,
        grid=(planes,),
        in_specs=[full, full] + tile_specs(groups),
        out_specs=[pl.BlockSpec((n, 1, rows, depth), lambda i: (0, i, 0, 0)), full],
        out_shape=[
            jax.ShapeDtypeStruct((n, planes, rows, depth), jnp.float32),
            jax.ShapeDtypeStruct((n, n), jnp.float32),
        ],
        scratch_shapes=[pltpu.VMEM((n, 4 * n), jnp.bfloat16)],
        compiler_params=pltpu.CompilerParams(vmem_limit_bytes=24 * MIB),
        cost_estimate=pl.CostEstimate(flops=0, bytes_accessed=8 * MIB, transcendentals=0),
        name="basis",
    )(a, b, *tiles)


def swap(value):
    return lax.ppermute(value, "gx", [(i, i ^ 1) for i in range(lax.axis_size("gx"))])


def relay(value):
    n = lax.axis_size("gx")
    return lax.ppermute(value, "gx", [(i, i + 2 - 4 * (i % 2)) for i in range(n) if 0 <= i + 2 - 4 * (i % 2) < n])


def above(value):
    n = lax.axis_size("gy")
    return lax.ppermute(value, "gy", [(i, i + 1) for i in range(n - 1)])


def below(value):
    n = lax.axis_size("gy")
    return lax.ppermute(value, "gy", [(i + 1, i) for i in range(n - 1)])


def summed(value):
    steps = []
    for axis in ("gy", "gx"):
        n = lax.axis_size(axis)
        assert n & (n - 1) == 0
        shift = 1
        while shift < n:
            steps.append((axis, shift, n))
            shift *= 2
    other = None
    for axis, shift, n in steps:
        if other is not None:
            value = value + other
        other = lax.ppermute(value, axis, [(i, i ^ shift) for i in range(n)])
    return value, other


def part_to_relay(side, recv, size, planes):
    fields = recv.reshape(size, planes, -1, recv.shape[-1])
    part = lax.dynamic_slice_in_dim(fields, (1 - side) * (planes - DEPTH), DEPTH, 1)
    return part.reshape(-1, recv.shape[-1])


def once(value, after):
    return value if after is None else lax.optimization_barrier((value, after))[0]


def body(probes, permeability, absorption, sensitivity, observe_weight):
    count, planes, rows, depth = probes.shape
    totals = (planes * lax.axis_size("gx"), rows * lax.axis_size("gy"))
    gx, gy = lax.axis_index("gx"), lax.axis_index("gy")
    side = gx % 2
    flag = side.reshape(1).astype(jnp.int32)
    at = jnp.stack([gx * planes - RING, gy * rows - EDGE]).astype(jnp.int32)
    assert 8 * sum(GROUPS) == count

    coef, parts = None, []
    groups, low = [], None
    tile = 0
    for number, size in enumerate(GROUPS):
        sizes = (size, planes, rows, 8)
        own = once(prep(probes, tile, size), parts[-2] if len(parts) > 1 else None)
        tile += size
        recv = swap(own)
        if number == 0:
            ext, first, wide = widened(side, (permeability, absorption, sensitivity, observe_weight), own)
            parts.append(first)
        part = part_to_relay(side, once(recv, (ylo, yhi, coef) if number == 1 else low), size, planes)
        parts.append(part)
        outer = relay(part)
        after = AFTER[number]
        low, high = border(flag, sizes, own, recv, outer, wide if after is None else groups[after])
        ylo, yhi = above(low), below(high)
        if number == 0:
            coef = coefficients(at, totals, once(ext, low))
        here = coef if number == 0 else once(coef, groups[-1])
        groups.append(solve(flag, sizes, here, own, recv, outer, ylo, yhi))
    a, b = summed(gram_of(groups, totals[0] * totals[1] * depth))
    q, r = basis(a, b, groups)
    return (q, r)


def solution(mesh):
    return jax.shard_map(
        body,
        mesh=mesh,
        in_specs=(
            P(None, "gx", "gy", None),
            P("gx", "gy", None),
            P("gx", "gy", None),
            P("gx", "gy", None),
            P("gx", "gy", None),
        ),
        out_specs=(P(None, "gx", "gy", None), P()),
        check_vma=False,
    )
```

```python
import functools

import jax
import jax.numpy as jnp
from jax import lax
from jax.experimental import pallas as pl
from jax.experimental.pallas import tpu as pltpu
from jax.sharding import PartitionSpec as P

OMEGA = 0.8
KEEP = 1.0 - OMEGA
A0 = 1.0 + KEEP + KEEP**2 + KEEP**3
A1 = 1.0 + 2.0 * KEEP + 3.0 * KEEP**2
A2 = 1.0 + 3.0 * KEEP
A3 = 1.0
DEPTH = 6
RING = DEPTH + 1
EDGE = 8
GROUPS = (1, 2, 2, 2, 1)
AFTER = (None, 0, 1, 1, 2)
BLOCK = 4
MIB = 1 << 20


def smem():
    return pl.BlockSpec(memory_space=pltpu.SMEM)


def vmem():
    return pl.BlockSpec(memory_space=pltpu.VMEM)


def prep_kernel(probes, out, wide):
    many, planes, rows, depth = probes.shape
    cells = planes * rows
    wide[...] = probes[...].astype(jnp.float32).reshape(wide.shape)

    def plane(x, carry):
        at = x * rows
        for y in range(rows):
            out[pl.ds(pl.multiple_of((at + y) * many, many), many), :] = wide[pl.ds(at + y, many, stride=cells), :]
        return carry

    lax.fori_loop(0, planes, plane, 0)


def prep(probes, tile, size):
    planes, rows, depth = probes.shape[1:]
    count = planes * rows * 8
    return pl.pallas_call(
        prep_kernel,
        grid=(size,),
        in_specs=[pl.BlockSpec((8, planes, rows, depth), lambda i: (tile + i, 0, 0, 0))],
        out_specs=pl.BlockSpec((count, depth), lambda i: (i, 0)),
        out_shape=jax.ShapeDtypeStruct((size * count, depth), jnp.float32),
        scratch_shapes=[pltpu.VMEM((count, depth), jnp.float32)],
        compiler_params=pltpu.CompilerParams(vmem_limit_bytes=40 * MIB),
        cost_estimate=pl.CostEstimate(flops=0, bytes_accessed=size * MIB, transcendentals=0),
        name="spread_probes",
    )(probes)


def pieces_of(side, tiles, planes, rows, many, own, recv, outer):
    depth = own.shape[-1]
    own, recv = (ref.reshape(tiles, planes, rows, many, depth) for ref in (own, recv))
    outer = outer.reshape(tiles, DEPTH, rows, many, depth)
    top = DEPTH + planes
    return (
        (own, 0, planes, 0, DEPTH),
        (recv, side * (planes - DEPTH), DEPTH, planes, top * (1 - side)),
        (outer, 0, DEPTH, planes + DEPTH, top * side),
    )


def border_kernel(sizes, h_ref, own, recv, outer, after, low, high):
    tiles, planes, rows, many = sizes
    shape = (tiles, planes + 2 * DEPTH, DEPTH, many, own.shape[-1])
    low, high = low.reshape(shape), high.reshape(shape)
    for piece, first, count, role, _ in pieces_of(h_ref[0], *sizes, own, recv, outer):
        for t in range(tiles):
            for i in range(count):
                low[t, role + i] = piece[t, first + i, rows - DEPTH :]
                high[t, role + i] = piece[t, first + i, :DEPTH]


def border(side, sizes, own, recv, outer, after):
    tiles, planes, rows, many = sizes
    message = jax.ShapeDtypeStruct((tiles * (planes + 2 * DEPTH) * DEPTH * many, own.shape[-1]), jnp.float32)
    return pl.pallas_call(
        functools.partial(border_kernel, sizes),
        in_specs=[smem()] + [vmem()] * 3 + [pl.BlockSpec(memory_space=pl.ANY)],
        out_specs=[vmem(), vmem()],
        out_shape=[message, message],
        compiler_params=pltpu.CompilerParams(vmem_limit_bytes=12 * MIB),
        cost_estimate=pl.CostEstimate(flops=0, bytes_accessed=2 * MIB, transcendentals=0),
        name="border_rows",
    )(side, own, recv, outer, after)


def coef_kernel(total_x, total_y, at_ref, ext, out, root):
    wide_x, wide_y, depth = root.shape
    y = at_ref[1] + lax.broadcasted_iota(jnp.int32, (wide_y, depth), 0)
    z = lax.broadcasted_iota(jnp.int32, (wide_y, depth), 1)
    inside = (y >= 0) & (y < total_y)
    root[0] = jnp.zeros((wide_y, depth), jnp.float32)
    root[wide_x - 1] = jnp.zeros((wide_y, depth), jnp.float32)

    def roots(i, carry):
        for x in (2 * i + 1, 2 * i + 2):
            k = ext[0, x]
            beside = ext[0, x - 1] + ext[0, x + 1] + pltpu.roll(k, 1, 0) + pltpu.roll(k, wide_y - 1, 0)
            beside = beside + jnp.where(z == 0, 0.0, pltpu.roll(k, 1, 1))
            beside = beside + jnp.where(z == depth - 1, 0.0, pltpu.roll(k, depth - 1, 1))
            diag = ext[1, x] + 0.5 * (6.0 * k + beside)
            here = inside & (at_ref[0] + x >= 0) & (at_ref[0] + x < total_x)
            root[x] = jnp.where(here, lax.rsqrt(jnp.where(here, diag, 1.0)), 0.0)
        return carry

    lax.fori_loop(0, (wide_x - 2) // 2, roots, 0)

    def plane(i, carry):
        for x in (2 * i + 1, 2 * i + 2):
            k, inv = ext[0, x], root[x]
            half = 0.5 * OMEGA * inv
            out[0, x] = half * root[x + 1] * (k + ext[0, x + 1])
            out[1, x] = half * pltpu.roll(inv, wide_y - 1, 0) * (k + pltpu.roll(k, wide_y - 1, 0))
            up = half * pltpu.roll(inv, depth - 1, 1) * (k + pltpu.roll(k, depth - 1, 1))
            out[2, x] = jnp.where(z == depth - 1, 0.0, up)
            out[3, x] = OMEGA * inv * ext[2, x]
            out[4, x] = (OMEGA * A0) * inv * inv * ext[3, x]
            out[5, x] = A0 * inv * ext[2, x]
        return carry

    lax.fori_loop(0, (wide_x - 2) // 2, plane, 0)


def widened(side, maps, after):
    planes, rows, depth = maps[0].shape
    lower = side == 0
    own = once(jnp.stack(maps), after)
    recv = swap(own)
    outer = relay(lax.dynamic_slice_in_dim(recv, (1 - side) * (planes - RING), RING, 1))
    inner = lax.dynamic_slice_in_dim(recv, side * (planes - RING), RING, 1)
    wide = jnp.concatenate([jnp.where(lower, outer, inner), own, jnp.where(lower, inner, outer)], axis=1)
    low, high = above(wide[:, :, rows - EDGE :]), below(wide[:, :, :EDGE])
    return jnp.concatenate([low, wide, high], axis=2), recv, wide


def coefficients(at, totals, ext):
    shape = ext.shape[1:]
    return pl.pallas_call(
        functools.partial(coef_kernel, *totals),
        in_specs=[smem(), vmem()],
        out_specs=vmem(),
        out_shape=jax.ShapeDtypeStruct((6,) + shape, jnp.float32),
        scratch_shapes=[pltpu.VMEM(shape, jnp.float32)],
        compiler_params=pltpu.CompilerParams(vmem_limit_bytes=12 * MIB),
        cost_estimate=pl.CostEstimate(flops=0, bytes_accessed=4 * MIB, transcendentals=0),
        name="coefficients",
    )(at, ext)


def spread(coef, which, x, y, many):
    return coef[which, x, pl.ds(y, many, stride=0), :]


def solve_kernel(sizes, h_ref, coef, own, recv, outer, ylo, yhi, out_ref, r_s, a_s, b_s):
    tiles, planes, rows, many = sizes
    wide_x, wide_y, _, depth = r_s.shape[1:]
    span = range(tiles)
    shape = (tiles, wide_x, DEPTH, many, depth)
    ylo, yhi = ylo.reshape(shape), yhi.reshape(shape)

    def row(which, x, y):
        return spread(coef, which, x + RING - DEPTH, y + EDGE - DEPTH, many)

    for piece, first, count, role, place in pieces_of(h_ref[0], *sizes, own, recv, outer):

        def fill(i, carry, piece=piece, first=first, role=role, place=place):
            x = place + i
            for y in range(wide_y):
                scale = row(3, x, y)
                for t in span:
                    if y < DEPTH:
                        value = ylo[t, role + i, y]
                    elif y < DEPTH + rows:
                        value = piece[t, first + i, y - DEPTH]
                    else:
                        value = yhi[t, role + i, y - DEPTH - rows]
                    r_s[t, x, y] = value * scale
            return carry

        lax.fori_loop(0, count, fill, 0)

    def stencil(src, r, x, block, low, scale, last=None):
        inner = range(block)
        prev = [[src[t, x + k, low - 1] for t in span] for k in inner]
        here = [[src[t, x + k, low] for t in span] for k in inner]
        cy_prev = [row(1, x + k, low - 1) for k in inner]
        for y in range(low, wide_y - low):
            after = [[src[t, x + k, y + 1] for t in span] for k in inner]
            cx = [row(0, x + k, y) for k in range(-1, block)]
            cy = [row(1, x + k, y) for k in inner]
            values = []
            for k in inner:
                cz = row(2, x + k, y)
                end = None if last is None else row(last, x + k, y)
                for t in span:
                    f = here[k][t]
                    before = here[k - 1][t] if k else src[t, x - 1, y]
                    beyond = here[k + 1][t] if k + 1 < block else src[t, x + block, y]
                    total = cx[k] * before + cx[k + 1] * beyond
                    total = total + (cy_prev[k] * prev[k][t] + cy[k] * after[k][t])
                    total = total + (pltpu.roll(cz * f, 1, 1) + cz * pltpu.roll(f, depth - 1, 1))
                    value = r[t, x + k, y] + scale * total
                    values.append((t, k, value if end is None else value * end))
            yield y, values
            prev, here, cy_prev = here, after, cy

    def sweep(src, dst, r, low, scale, last=None):
        def planes_at(x, block):
            for y, values in stencil(src, r, x, block, low, scale, last):
                for t, k, value in values:
                    dst[t, x + k, y] = value

        def step(i, carry):
            planes_at(low + BLOCK * i, BLOCK)
            return carry

        full, rest = divmod(wide_x - 2 * low, BLOCK)
        lax.fori_loop(0, full, step, 0)
        if rest:
            planes_at(low + BLOCK * full, rest)

    sweep(r_s, a_s, r_s, 1, A3 / A2)
    sweep(a_s, b_s, r_s, 2, A2 / A1)
    sweep(b_s, a_s, r_s, 3, A1 / A0, last=4)
    sweep(a_s, b_s, a_s, 4, A3 / A2)
    sweep(b_s, r_s, a_s, 5, A2 / A1)

    def out(i, carry):
        for y, values in stencil(r_s, a_s, DEPTH + BLOCK * i, BLOCK, DEPTH, A1 / A0, last=5):
            for t, k, value in values:
                out_ref[t, BLOCK * i + k, y - DEPTH] = value
        return carry

    lax.fori_loop(0, planes // BLOCK, out, 0)


def solve(side, sizes, coef, *messages):
    tiles, planes, rows, many = sizes
    depth = coef.shape[-1]
    wide = (planes + 2 * DEPTH, rows + 2 * DEPTH)
    field = pltpu.VMEM((tiles,) + wide + (many, depth), jnp.float32)
    cells = tiles * wide[0] * wide[1] * many * depth
    return pl.pallas_call(
        functools.partial(solve_kernel, sizes),
        in_specs=[smem()] + [vmem()] * 6,
        out_specs=vmem(),
        out_shape=jax.ShapeDtypeStruct((tiles, planes, rows, many, depth), jnp.float32),
        scratch_shapes=[field, field, field],
        compiler_params=pltpu.CompilerParams(vmem_limit_bytes=(6 + 12 * tiles) * MIB),
        cost_estimate=pl.CostEstimate(flops=60 * cells, bytes_accessed=12 * MIB, transcendentals=0),
        name="both_solves",
    )(side, coef, *messages)


def stacked(tiles, rows):
    columns = [jnp.concatenate([t[0, 0, y] for t in tiles], axis=0) for y in range(rows)]
    return jnp.concatenate(columns, axis=1)


def split(value):
    high = value.astype(jnp.bfloat16)
    return high, (value - high.astype(jnp.float32)).astype(jnp.bfloat16)


def gram_kernel(scale, *refs):
    tiles, out, total = refs[:-2], refs[-2], refs[-1]
    step = pl.program_id(0)

    @pl.when(step == 0)
    def _():
        total[...] = jnp.zeros_like(total)

    both = jnp.concatenate(split(stacked(tiles, tiles[0].shape[2])), axis=0)
    total[...] += lax.dot_general(both, both, (((1,), (1,)), ((), ())), preferred_element_type=jnp.float32)

    @pl.when(step == pl.num_programs(0) - 1)
    def _():
        n = out.shape[0]
        g = total[:n, :n] + total[:n, n:] + total[n:, :n] + total[n:, n:]
        out[...] = g * scale


def tile_specs(groups):
    return [
        pl.BlockSpec((1, 1) + g.shape[2:], lambda i, t=t: (t, i, 0, 0, 0)) for g in groups for t in range(g.shape[0])
    ]


def tile_args(groups):
    return [g for g in groups for t in range(g.shape[0])]


def gram_of(groups, cells):
    tiles = tile_args(groups)
    count = 8 * len(tiles)
    return pl.pallas_call(
        functools.partial(gram_kernel, 1.0 / cells),
        grid=(tiles[0].shape[1],),
        in_specs=tile_specs(groups),
        out_specs=pl.BlockSpec((count, count), lambda i: (0, 0)),
        out_shape=jax.ShapeDtypeStruct((count, count), jnp.float32),
        scratch_shapes=[pltpu.VMEM((2 * count, 2 * count), jnp.float32)],
        compiler_params=pltpu.CompilerParams(vmem_limit_bytes=16 * MIB),
        cost_estimate=pl.CostEstimate(flops=0, bytes_accessed=6 * MIB, transcendentals=0),
        name="gram",
    )(*tiles)


def factor(gram):
    n = gram.shape[0]
    i = lax.broadcasted_iota(jnp.int32, (n, n), 0)
    j = lax.broadcasted_iota(jnp.int32, (n, n), 1)
    both = jnp.concatenate([gram, (i == j).astype(jnp.float32)], axis=1)
    rows = [both[8 * t : 8 * t + 8] for t in range(n // 8)]
    place = lax.broadcasted_iota(jnp.int32, (8, 2 * n), 0)
    for c in range(0, n, 2):
        t, s = divmod(c, 8)
        first, second = rows[t][s : s + 1], rows[t][s + 1 : s + 2]
        a, b, d = first[:, c : c + 1], first[:, c + 1 : c + 2], second[:, c + 1 : c + 2]
        inv = 1.0 / (a * d - b * b)
        w1 = (d * first - b * second) * inv
        w2 = (a * second - b * first) * inv
        fixed = jnp.where(place == s + 1, second - (b / a) * first, rows[t])
        for k in range(t, n // 8):
            new = rows[k] - (rows[k][:, c : c + 1] * w1 + rows[k][:, c + 1 : c + 2] * w2)
            rows[k] = jnp.where(place > s + 1, new, fixed) if k == t else new
    done = jnp.concatenate(rows, axis=0)
    size = jnp.sum(jnp.where(i == j, done[:, :n], 0.0), axis=1, keepdims=True)
    done = done * lax.rsqrt(size)
    return done[:, :n], done[:, n:]


def basis_kernel(a_ref, b_ref, *refs):
    tiles, (q_ref, r_ref, left) = refs[:-3], refs[-3:]
    n = r_ref.shape[0]
    rows = tiles[0].shape[2]

    @pl.when(pl.program_id(0) == 0)
    def _():
        upper, inverse = factor(a_ref[...] + b_ref[...])
        i = lax.broadcasted_iota(jnp.int32, (n, n), 0)
        j = lax.broadcasted_iota(jnp.int32, (n, n), 1)
        r_ref[...] = jnp.where(j >= i, upper, 0.0)
        inverse = jnp.where(j <= i, inverse, 0.0)
        high, low = split(inverse)
        left[...] = jnp.concatenate([high, high, low, low], axis=1)

    high, low = split(stacked(tiles, rows))
    q = jnp.dot(left[...], jnp.concatenate([high, low, high, low], axis=0), preferred_element_type=jnp.float32)
    depth = q.shape[1] // rows
    flat = q_ref.reshape(n * rows, depth)
    for y in range(rows):
        flat[pl.ds(y, n, stride=rows), :] = q[:, y * depth : (y + 1) * depth]


def basis(a, b, groups):
    n = a.shape[0]
    tiles = tile_args(groups)
    _, planes, rows, _, depth = tiles[0].shape
    full = pl.BlockSpec((n, n), lambda i: (0, 0))
    return pl.pallas_call(
        basis_kernel,
        grid=(planes,),
        in_specs=[full, full] + tile_specs(groups),
        out_specs=[pl.BlockSpec((n, 1, rows, depth), lambda i: (0, i, 0, 0)), full],
        out_shape=[
            jax.ShapeDtypeStruct((n, planes, rows, depth), jnp.float32),
            jax.ShapeDtypeStruct((n, n), jnp.float32),
        ],
        scratch_shapes=[pltpu.VMEM((n, 4 * n), jnp.bfloat16)],
        compiler_params=pltpu.CompilerParams(vmem_limit_bytes=24 * MIB),
        cost_estimate=pl.CostEstimate(flops=0, bytes_accessed=8 * MIB, transcendentals=0),
        name="basis",
    )(a, b, *tiles)


def swap(value):
    return lax.ppermute(value, "gx", [(i, i ^ 1) for i in range(lax.axis_size("gx"))])


def relay(value):
    n = lax.axis_size("gx")
    return lax.ppermute(value, "gx", [(i, i + 2 - 4 * (i % 2)) for i in range(n) if 0 <= i + 2 - 4 * (i % 2) < n])


def above(value):
    n = lax.axis_size("gy")
    return lax.ppermute(value, "gy", [(i, i + 1) for i in range(n - 1)])


def below(value):
    n = lax.axis_size("gy")
    return lax.ppermute(value, "gy", [(i + 1, i) for i in range(n - 1)])


def summed(value):
    steps = []
    for axis in ("gy", "gx"):
        n = lax.axis_size(axis)
        assert n & (n - 1) == 0
        shift = 1
        while shift < n:
            steps.append((axis, shift, n))
            shift *= 2
    other = None
    for axis, shift, n in steps:
        if other is not None:
            value = value + other
        other = lax.ppermute(value, axis, [(i, i ^ shift) for i in range(n)])
    return value, other


def part_to_relay(side, recv, size, planes):
    fields = recv.reshape(size, planes, -1, recv.shape[-1])
    part = lax.dynamic_slice_in_dim(fields, (1 - side) * (planes - DEPTH), DEPTH, 1)
    return part.reshape(-1, recv.shape[-1])


def once(value, after):
    return value if after is None else lax.optimization_barrier((value, after))[0]


def body(probes, permeability, absorption, sensitivity, observe_weight):
    count, planes, rows, depth = probes.shape
    totals = (planes * lax.axis_size("gx"), rows * lax.axis_size("gy"))
    gx, gy = lax.axis_index("gx"), lax.axis_index("gy")
    side = gx % 2
    flag = side.reshape(1).astype(jnp.int32)
    at = jnp.stack([gx * planes - RING, gy * rows - EDGE]).astype(jnp.int32)
    assert 8 * sum(GROUPS) == count

    coef, parts = None, []
    groups, low, ylo, yhi = [], None, None, None
    tile = 0
    for number, size in enumerate(GROUPS):
        sizes = (size, planes, rows, 8)
        own = once(prep(probes, tile, size), parts[-2] if len(parts) > 1 else None)
        tile += size
        recv = swap(own)
        if number == 0:
            ext, first, wide = widened(side, (permeability, absorption, sensitivity, observe_weight), own)
            parts.append(first)
        before = {1: (ylo, yhi, coef), 3: groups[1] if number == 3 else None}.get(number, low)
        part = part_to_relay(side, once(recv, before), size, planes)
        parts.append(part)
        outer = relay(part)
        after = AFTER[number]
        low, high = border(flag, sizes, own, recv, outer, wide if after is None else groups[after])
        ylo, yhi = above(low), below(high)
        if number == 0:
            coef = coefficients(at, totals, once(ext, low))
        here = coef if number == 0 else once(coef, groups[-1])
        groups.append(solve(flag, sizes, here, own, recv, outer, ylo, yhi))
    a, b = summed(gram_of(groups, totals[0] * totals[1] * depth))
    q, r = basis(a, b, groups)
    return (q, r)


def solution(mesh):
    return jax.shard_map(
        body,
        mesh=mesh,
        in_specs=(
            P(None, "gx", "gy", None),
            P("gx", "gy", None),
            P("gx", "gy", None),
            P("gx", "gy", None),
            P("gx", "gy", None),
        ),
        out_specs=(P(None, "gx", "gy", None), P()),
        check_vma=False,
    )
```
